128 devices in a mesh: tm: 128 (over z, y, x, core).
Axes of the slice: x: 4, y: 4, z: 4, core: 2. Of those that a mesh axis runs over, the one named last changes fastest.
Arguments:
- hidden: bfloat16 [49152, 8192], P('tm'), may hold values from -6 to 6
- norm_gain: float32 [8192], replicated, may hold values from 0.1 to 1.9
- w_in: bfloat16 [8192, 768], replicated, may hold values from -0.0625 to 0.0625
- w_short: float32 [768, 7], replicated, may hold values from -2 to 2
- residues: float32 [8, 16], replicated, may hold values from -4 to 4
- rates: float32 [8, 16], replicated, may hold values from 4.06901042e-06 to 0.0333333333, as said below
- skip: float32 [256], replicated, may hold values from -4 to 4
- w_out: bfloat16 [256, 8192], replicated, may hold values from -0.375 to 0.375
Outputs:
- mixed: bfloat16 [49152, 8192], P('tm')
The draws below stay inside these ranges and needn't reach their ends.
Inputs may be any that keep to these rules, and one draw needn't show every extreme that they name: `rates`: every rate is positive.
All inputs are finite; a program needn't handle non-finite values.
Results may differ from the reference program's by a relative error of at most 0.0088.
Values may be sent and summed in bfloat16 or wider, within the bound.
No kernel may reach another device: no remote copies, remote signals or barrier semaphores. Data moves between devices by JAX's collectives and lax.ppermute only.
A program may use at most 256 MiB of HBM per device.

```python
import jax
import jax.numpy as jnp
from jax import lax

D = 8192
C = 32
GROUPS = 8
M = 16
TAPS = 7
TOK_DEV = 384
CT = 256
TOKENS = 49152
N_TM = 128


def draw_rates(key, part):
    key_order = jax.random.fold_in(key, 11)
    key_slow = jax.random.fold_in(key, 12)
    key_fast = jax.random.fold_in(key, 13)
    order = jax.vmap(lambda sub: jax.random.permutation(sub, M))(jax.random.split(key_order, GROUPS))
    slow_low = jnp.log(0.2 / TOKENS)
    slow_high = jnp.log(2.0 / TOKENS)
    fast_low = jnp.log(1.0 / (2.0 * TOK_DEV))
    fast_high = jnp.log(1.0 / 30.0)
    slow_draw = slow_low + (slow_high - slow_low) * jax.random.uniform(key_slow, (GROUPS, M), jnp.float32)
    fast_draw = fast_low + (fast_high - fast_low) * jax.random.uniform(key_fast, (GROUPS, M), jnp.float32)
    slow_count = M // 2
    chosen = jnp.where(order < slow_count, slow_draw, fast_draw)
    return jnp.exp(chosen).astype(jnp.float32)


def shard_levels(own_key, dims, cuts, smallest, high):
    def one(dim, shards_of):
        heights = jax.random.uniform(jax.random.fold_in(jax.random.fold_in(own_key, 6), dim), (shards_of,), jnp.float32, smallest / len(cuts), high / len(cuts))
        return jnp.repeat(jnp.exp(heights), dims[dim] // shards_of).reshape((-1,) + (1,) * (len(dims) - dim - 1))

    loudness = one(*cuts[0])
    for cut in cuts[1:]:
        loudness = loudness * one(*cut)
    return loudness


def bell_draw(stream_key, shape, scale, most, cuts=(), held_as=jnp.bfloat16):
    drawn = jax.random.normal(stream_key, shape, jnp.float32) * scale
    if len(cuts) > 0:
        drawn = shard_levels(stream_key, shape, cuts, -0.22, 0.18) * drawn
    return jnp.clip(drawn, min=-most, max=most).astype(held_as)


def setup_inputs(seed: int = 0) -> dict:
    seeds = jax.random.split(jax.random.key(seed), 9)
    return {
        "hidden": bell_draw(seeds[0], (TOKENS, D), 1.0, 6.0, ((0, 128),)),
        "norm_gain": jnp.clip(1.0 + 0.18 * jax.random.normal(seeds[1], (D,), jnp.float32), 0.1, 1.9),
        "w_in": bell_draw(seeds[2], (D, 3 * CT), D ** -0.5, 0.0625),
        "w_short": bell_draw(seeds[3], (3 * CT, TAPS), TAPS ** -0.5, 2.0, (), jnp.float32),
        "residues": bell_draw(seeds[4], (GROUPS, M), 1.0, 4.0, (), jnp.float32),
        "rates": draw_rates(jax.random.fold_in(seeds[8], 71), 0),
        "skip": bell_draw(seeds[6], (CT,), 1.0, 4.0, (), jnp.float32),
        "w_out": bell_draw(seeds[7], (CT, D), CT ** -0.5, 0.375),
    }


def filter_taps(lag_values, rates, residues):
    weights = residues * jnp.sqrt(2.0 * rates)
    lagged = lag_values.astype(jnp.float32)
    values = lax.optimization_barrier(jnp.sum(weights * jnp.exp(-rates * jnp.maximum(lagged, 0.0)[..., None, None]), axis=-1))
    return jnp.where((lagged >= 0.0)[..., None], values, 0.0)

def reference(hidden, norm_gain, w_in, w_short, residues, rates, skip, w_out):

    def project_in(segment):
        widened = segment.astype(jnp.float32)
        inv_scale = lax.rsqrt(lax.optimization_barrier(jnp.mean(widened * widened, axis=1, keepdims=True)) + 1e-06)
        normed = (widened * inv_scale * norm_gain).astype(jnp.bfloat16)
        return jnp.dot(normed, w_in, preferred_element_type=jnp.float32).astype(jnp.bfloat16)
    projected = lax.map(project_in, hidden.reshape(N_TM, TOK_DEV, D)).reshape(TOKENS, 3 * CT)
    padded = jnp.concatenate([jnp.zeros((TAPS - 1, 3 * CT), jnp.bfloat16), projected], axis=0).astype(jnp.float32)
    features = jnp.zeros((TOKENS, 3 * CT), jnp.float32)
    for offset_tap in range(TAPS):
        features = features + w_short[:, offset_tap] * padded[TAPS - 1 - offset_tap:TAPS - 1 - offset_tap + TOKENS]
    queries = features[:, :CT]
    keyed = features[:, CT:2 * CT]
    valued = features[:, 2 * CT:]
    product = (keyed * valued).astype(jnp.bfloat16).astype(jnp.float32)
    filt = filter_taps(jnp.arange(TOKENS, dtype=jnp.int32), rates, residues)
    filt_channels = jnp.repeat(filt, C, axis=1)
    length = 2 * TOKENS
    spectrum = jnp.fft.rfft(filt_channels, n=length, axis=0) * jnp.fft.rfft(product, n=length, axis=0)
    convolved = jnp.fft.irfft(spectrum, n=length, axis=0)[:TOKENS].astype(jnp.float32)
    gated = (queries * (convolved + skip * product)).astype(jnp.bfloat16)

    def project_out(segment):
        return jnp.dot(segment, w_out, preferred_element_type=jnp.float32).astype(jnp.bfloat16)
    return lax.map(project_out, gated.reshape(N_TM, TOK_DEV, CT)).reshape(TOKENS, D)
```

```python
import jax
import jax.numpy as jnp
from jax import lax
from jax.experimental import pallas as pl
from jax.experimental.pallas import tpu as pltpu
from jax.sharding import PartitionSpec as P

F32 = jnp.float32
BF16 = jnp.bfloat16
HALO = 8
MIB = 1 << 20


def split(value):
    high = value.astype(BF16)
    return high, (value - high.astype(F32)).astype(BF16)


def dot(left, right):
    return jnp.dot(left, right, preferred_element_type=F32)


def project_kernel(hidden_ref, gain_ref, w_ref, out_ref, total, squares):
    step = pl.program_id(0)
    wide = hidden_ref[...].astype(F32)
    part = dot((wide * gain_ref[...]).astype(BF16), w_ref[...])
    power = jnp.sum((wide * wide).reshape(wide.shape[0], -1, 128), axis=1)

    @pl.when(step == 0)
    def _():
        total[...] = part
        squares[...] = power

    @pl.when(step > 0)
    def _():
        total[...] += part
        squares[...] += power

    @pl.when(step == pl.num_programs(0) - 1)
    def _():
        width = hidden_ref.shape[1] * pl.num_programs(0)
        mean = jnp.sum(squares[...], axis=1, keepdims=True) / width
        out_ref[...] = (total[...] * lax.rsqrt(mean + 1e-06)).astype(BF16)


def project(hidden, gain, w_in, block):
    rows, width = hidden.shape
    columns = w_in.shape[1]
    return pl.pallas_call(
        project_kernel,
        grid=(width // block,),
        in_specs=[
            pl.BlockSpec((rows, block), lambda k: (0, k)),
            pl.BlockSpec((1, block), lambda k: (0, k)),
            pl.BlockSpec((block, columns), lambda k: (k, 0)),
        ],
        out_specs=pl.BlockSpec((rows, columns), lambda k: (0, 0)),
        out_shape=jax.ShapeDtypeStruct((rows, columns), BF16),
        scratch_shapes=[pltpu.VMEM((rows, columns), F32), pltpu.VMEM((rows, 128), F32)],
        compiler_params=pltpu.CompilerParams(vmem_limit_bytes=16 * MIB),
        cost_estimate=pl.CostEstimate(
            flops=2 * rows * width * columns,
            bytes_accessed=2 * width * (rows + columns),
            transcendentals=0,
        ),
        name="project",
    )(hidden, gain, w_in)


def features_kernel(
    halo_ref, gain_ref, w_ref, proj_ref, taps_ref, rcol_ref, query_ref, prod_ref, state_ref, ext
):
    wide = halo_ref[...].astype(F32)
    width = wide.shape[1]
    rows, columns = proj_ref.shape
    chan = columns // 3
    inv = lax.rsqrt(jnp.mean(wide * wide, axis=1, keepdims=True) + 1e-06)
    edge = dot((wide * gain_ref[...]).astype(BF16), w_ref[...]) * inv
    ext[0:HALO, :] = edge.astype(BF16).astype(F32)
    ext[HALO : HALO + rows, :] = proj_ref[...].astype(F32)

    def feature(first):
        cols = slice(first, first + chan)
        total = taps_ref[0:1, cols] * ext[HALO : HALO + rows, cols]
        for k in range(1, taps_ref.shape[0]):
            total = total + taps_ref[k : k + 1, cols] * ext[HALO - k : HALO - k + rows, cols]
        return total

    query_ref[...] = feature(0)
    product = (feature(chan) * feature(2 * chan)).astype(BF16)
    prod_ref[...] = product
    spots = lax.broadcasted_iota(jnp.int32, (1, rows), 1)
    left = (rows - 1 - spots).astype(F32)
    high, low = split(jnp.exp(-rcol_ref[...] * left))
    crossed = dot(high, product) + dot(low, product)
    modes = state_ref.shape[0]
    groups = crossed.shape[0] // modes
    owner = lax.broadcasted_iota(jnp.int32, (modes, chan), 1) // (chan // groups)
    state = jnp.zeros((modes, chan), F32)
    for g in range(groups):
        state = jnp.where(owner == g, crossed[g * modes : (g + 1) * modes, :], state)
    state_ref[...] = state


def local_kernel(prod_ref, skip_ref, rcol_ref, wcol_ref, out_ref):
    rows, chan = prod_ref.shape
    block = 128
    blocks = rows // block
    span = (blocks + 1) * block
    modes = rcol_ref.shape[0] // groups_of(prod_ref)
    groups = groups_of(prod_ref)
    per = chan // groups
    top = (blocks - 1) * block
    spots = lax.broadcasted_iota(jnp.int32, (1, span), 1)
    lags = jnp.where(spots <= top, top - spots, top + span - spots)
    used = (spots <= top) | (spots > blocks * block)
    terms = wcol_ref[...] * jnp.exp(-rcol_ref[...] * lags.astype(F32))
    terms = jnp.where(used, terms, 0.0)
    for g in range(groups):
        filt = jnp.sum(terms[g * modes : (g + 1) * modes, :], axis=0, keepdims=True)
        wide = jnp.broadcast_to(filt, (block, span))
        strip = pltpu.roll(wide, 0, 1, stride=1, stride_axis=0)[:, : blocks * block].astype(BF16)
        cols = slice(g * per, (g + 1) * per)
        mine = prod_ref[:, cols]
        for i in range(blocks):
            near = strip[:, (blocks - 1 - i) * block :]
            conv = dot(near, mine[: (i + 1) * block])
            here = slice(i * block, (i + 1) * block)
            out_ref[here, cols] = conv + skip_ref[:, cols] * mine[here].astype(F32)


def groups_of(prod_ref):
    return prod_ref.shape[1] // 32


def prefix_kernel(chip_ref, all_ref, rate_ref, first_ref, mine_ref, next_ref, *, hop):
    count = all_ref.shape[0]
    fall = jnp.exp(-rate_ref[...] * (2.0 * hop))
    chip = chip_ref[0]

    def step(j, total):
        return jnp.where(j < chip, fall * total + all_ref[j].astype(F32), total)

    total = jnp.zeros(rate_ref.shape, F32)
    total = lax.fori_loop(0, count, step, total, unroll=8)
    mine_ref[...] = total
    next_ref[...] = jnp.exp(-rate_ref[...] * hop) * total + first_ref[...]


def mix_kernel(query_ref, base_ref, state_ref, rrow_ref, wrow_ref, w_ref, out_ref, gated):
    step = pl.program_id(0)

    @pl.when(step == 0)
    def _():
        rows, chan = query_ref.shape
        state = state_ref[...]
        modes = state.shape[0]
        groups = rrow_ref.shape[1] // modes
        owner = lax.broadcasted_iota(jnp.int32, (modes, chan), 1) // (chan // groups)
        spread = jnp.concatenate(
            [jnp.where(owner == g, state, 0.0) for g in range(groups)], axis=0
        )
        times = lax.broadcasted_iota(jnp.int32, (rows, 1), 0).astype(F32) + 1.0
        rising = wrow_ref[...] * jnp.exp(-rrow_ref[...] * times)
        rise_high, rise_low = split(rising)
        high, low = split(spread)
        carry = dot(rise_high, high) + dot(rise_low, high) + dot(rise_high, low)
        gated[...] = (query_ref[...] * (base_ref[...] + carry)).astype(BF16)

    out_ref[...] = dot(gated[...], w_ref[...]).astype(BF16)


def on_device(hidden, norm_gain, w_in, w_short, residues, rates, skip, w_out):
    rows, width = hidden.shape
    chan = w_short.shape[0] // 3
    half = chan // 2
    groups, modes = rates.shape
    devices = lax.axis_size("tm")
    here = lax.axis_index("tm")
    core = here % 2
    edge = lax.ppermute(hidden[rows - HALO :], "tm", [(i, i + 1) for i in range(devices - 1)])
    gain = norm_gain[None, :]
    weights = residues * jnp.sqrt(2.0 * rates)
    rcol, wcol = rates.reshape(-1, 1), weights.reshape(-1, 1)
    rrow, wrow = rates.reshape(1, -1), weights.reshape(1, -1)
    taps = w_short.T
    rate_chan = jnp.repeat(rates.T, chan // groups, axis=1)
    rate_half = lax.dynamic_slice_in_dim(rate_chan, core * half, half, axis=1)

    projected = project(hidden, gain, w_in, 1024)
    query, product, state = pl.pallas_call(
        features_kernel,
        out_shape=[
            jax.ShapeDtypeStruct((rows, chan), F32),
            jax.ShapeDtypeStruct((rows, chan), BF16),
            jax.ShapeDtypeStruct((modes, chan), F32),
        ],
        scratch_shapes=[pltpu.VMEM((rows + HALO, 3 * chan), F32)],
        compiler_params=pltpu.CompilerParams(vmem_limit_bytes=32 * MIB),
        cost_estimate=pl.CostEstimate(
            flops=2 * HALO * width * 3 * chan, bytes_accessed=2 * width * 3 * chan, transcendentals=0
        ),
        name="features",
    )(edge, gain, w_in, projected, taps, rcol)

    base = pl.pallas_call(
        local_kernel,
        out_shape=jax.ShapeDtypeStruct((rows, chan), F32),
        compiler_params=pltpu.CompilerParams(vmem_limit_bytes=16 * MIB),
        cost_estimate=pl.CostEstimate(
            flops=2 * rows * rows * chan, bytes_accessed=6 * rows * chan, transcendentals=0
        ),
        name="local",
    )(product, skip[None, :], rcol, wcol)

    pairs = [(i, i ^ 1) for i in range(devices)]
    own = lax.dynamic_slice_in_dim(state, core * half, half, axis=1)
    other = lax.dynamic_slice_in_dim(state, (1 - core) * half, half, axis=1)
    got = lax.ppermute(other, "tm", pairs)
    first = jnp.where(core == 0, own, got)
    second = jnp.where(core == 0, got, own)
    chip_state = (jnp.exp(-rate_half * rows) * first + second).astype(BF16)
    members = [list(range(c, devices, 2)) for c in range(2)]
    spread = lax.all_to_all(
        jnp.broadcast_to(chip_state, (devices // 2,) + chip_state.shape),
        "tm",
        0,
        0,
        tiled=True,
        axis_index_groups=members,
    )
    mine, following = pl.pallas_call(
        lambda *refs: prefix_kernel(*refs, hop=float(rows)),
        in_specs=[pl.BlockSpec(memory_space=pltpu.SMEM)] + [pl.BlockSpec(memory_space=pltpu.VMEM)] * 3,
        out_shape=[jax.ShapeDtypeStruct((modes, half), F32)] * 2,
        compiler_params=pltpu.CompilerParams(vmem_limit_bytes=8 * MIB),
        name="prefix",
    )((here // 2).astype(jnp.int32)[None], spread, rate_half, first)
    back = lax.ppermute(jnp.where(core == 0, following, mine), "tm", pairs)
    keep = jnp.where(core == 0, mine, following)
    before = jnp.where(
        core == 0,
        jnp.concatenate([keep, back], axis=1),
        jnp.concatenate([back, keep], axis=1),
    )

    block = 1024
    out_width = w_out.shape[1]
    return pl.pallas_call(
        mix_kernel,
        grid=(out_width // block,),
        in_specs=[
            pl.BlockSpec((rows, chan), lambda n: (0, 0)),
            pl.BlockSpec((rows, chan), lambda n: (0, 0)),
            pl.BlockSpec((modes, chan), lambda n: (0, 0)),
            pl.BlockSpec((1, groups * modes), lambda n: (0, 0)),
            pl.BlockSpec((1, groups * modes), lambda n: (0, 0)),
            pl.BlockSpec((chan, block), lambda n: (0, n)),
        ],
        out_specs=pl.BlockSpec((rows, block), lambda n: (0, n)),
        out_shape=jax.ShapeDtypeStruct((rows, out_width), BF16),
        scratch_shapes=[pltpu.VMEM((rows, chan), BF16)],
        compiler_params=pltpu.CompilerParams(vmem_limit_bytes=16 * MIB),
        name="mix",
    )(query, base, before, rrow, wrow, w_out)


def solution(mesh):
    return jax.shard_map(
        on_device,
        mesh=mesh,
        in_specs=(P("tm", None), P(), P(), P(), P(), P(), P(), P()),
        out_specs=P("tm", None),
        check_vma=False,
    )
```

```python
import functools

import jax
import jax.numpy as jnp
from jax import lax
from jax.experimental import pallas as pl
from jax.experimental.pallas import tpu as pltpu
from jax.sharding import PartitionSpec as P

F32 = jnp.float32
BF16 = jnp.bfloat16
HALO = 8
MIB = 1 << 20


def split(value):
    high = value.astype(BF16)
    return high, (value - high.astype(F32)).astype(BF16)


def dot(left, right):
    return jnp.dot(left, right, preferred_element_type=F32)


def spot(axis, count):
    shape = (1, count) if axis else (count, 1)
    return lax.broadcasted_iota(jnp.int32, shape, axis)


def copies(source, target, axis, count, sems):
    size = source.shape[axis] // count
    made = []
    for k in range(count):
        part = pl.ds(k * size, size)
        index = (part, slice(None)) if axis == 0 else (slice(None), part)
        made.append(pltpu.make_async_copy(source.at[index], target.at[index], sems.at[k]))
    return made


def column(table):
    groups, modes = table.shape
    rows = jnp.concatenate(
        [jnp.broadcast_to(table[g : g + 1, :], (modes, modes)) for g in range(groups)], axis=0
    )
    mine = spot(1, modes) == lax.rem(spot(0, groups * modes), modes)
    return jnp.sum(jnp.where(mine, rows, 0.0), axis=1, keepdims=True)


def fold(stacked, modes, per):
    width = stacked.shape[1]
    owner = spot(1, width) // per
    total = jnp.zeros((modes, width), F32)
    for g in range(stacked.shape[0] // modes):
        total = jnp.where(owner == g, stacked[g * modes : (g + 1) * modes, :], total)
    return total


def by_channel(col, modes, per, width):
    return fold(jnp.broadcast_to(col, (col.shape[0], width)), modes, per)


def feature(taps, ext, rows, first, width, at=0):
    cols = slice(at, at + width)
    wide = slice(first, first + width)
    total = taps[0:1, wide] * ext[HALO : HALO + rows, cols]
    for k in range(1, taps.shape[0]):
        total = total + taps[k : k + 1, wide] * ext[HALO - k : HALO - k + rows, cols]
    return total


def multiply(hidden, inv, gain, near, total, weights, store):
    rows = hidden.shape[0]
    count = len(weights)
    block = near.shape[0] // count
    part = rows // 3
    for k in range(count):
        weights[k].wait()
        cols = slice(k * block, (k + 1) * block)
        for first in range(0, rows, part):
            here = slice(first, first + part)
            scale = jnp.concatenate([inv[here, :]] * (block // 128), axis=1)
            normed = (hidden[here, cols].astype(F32) * scale * gain[:, cols]).astype(BF16)
            made = dot(normed, near[cols, :])
            if k == 0:
                total[here, :] = made
            elif k + 1 < count:
                total[here, :] += made
            else:
                store(here, (total[here, :] + made).astype(BF16))


def state_kernel(
    place_ref, hidden_hbm, gain_hbm, w_hbm, taps_hbm, rates_hbm,
    prod_ref, inv_ref, edge_ref, own_ref, other_ref,
    hidden, near, gain, taps, rates, total, ext, little, sems,
):
    rows, width = hidden.shape
    chan = prod_ref.shape[1]
    reach = taps.shape[0] - 1
    small = [
        pltpu.make_async_copy(source, target, sems.at[2, k])
        for k, (source, target) in enumerate(
            ((gain_hbm, gain), (taps_hbm, taps), (rates_hbm, rates))
        )
    ]
    lines = copies(hidden_hbm, hidden, 1, 4, sems.at[0])
    weights = copies(w_hbm.at[:, pl.ds(chan, 2 * chan)], near, 0, 8, sems.at[1])
    for copy in lines + small:
        copy.start()
    inv_ref[...] = jnp.zeros_like(inv_ref)
    block = width // len(lines)
    for k, copy in enumerate(lines):
        copy.wait()
        weights[2 * k].start()
        weights[2 * k + 1].start()

        def add(i, _, k=k):
            cols = pl.ds(pl.multiple_of(k * block + i * 256, 256), 256)
            wide = hidden[:, cols].astype(F32)
            square = wide * wide
            inv_ref[...] += square[:, :128] + square[:, 128:]
            return 0

        lax.fori_loop(0, block // 256, add, 0)
    inv = lax.rsqrt(jnp.sum(inv_ref[...], axis=1, keepdims=True) / width + 1e-06)
    inv_ref[...] = jnp.broadcast_to(inv, inv_ref.shape)
    for copy in small:
        copy.wait()

    def store(here, value):
        ext[HALO + here.start : HALO + here.stop, :] = value.astype(F32)

    ext[0:HALO, :] = jnp.zeros((HALO, 2 * chan), F32)
    multiply(hidden, inv_ref, gain, near, total, weights, store)

    head_k = feature(taps, ext, rows, chan, chan, 0)
    head_v = feature(taps, ext, rows, 2 * chan, chan, chan)
    later = spot(0, rows) >= reach
    product = jnp.where(later, head_k * head_v, 0.0).astype(BF16)
    prod_ref[...] = product
    edge_ref[0:HALO, :] = ext[HALO : 2 * HALO, :]
    edge_ref[HALO:, :] = ext[rows : rows + HALO, :]
    little[0:HALO, :] = ext[rows : rows + HALO, :]
    little[HALO:, :] = jnp.zeros((HALO, 2 * chan), F32)
    tail_k = feature(taps, little, HALO, chan, chan, 0)
    tail_v = feature(taps, little, HALO, 2 * chan, chan, chan)
    early = spot(0, HALO) < reach
    head_k = jnp.where(early, head_k[0:HALO, :], 0.0)
    head_v = jnp.where(early, head_v[0:HALO, :], 0.0)

    modes = rates.shape[1]
    left = (rows - 1 - spot(1, rows)).astype(F32)
    high, low = split(jnp.exp(-column(rates[...]) * left))
    state = fold(dot(high, product) + dot(low, product), modes, chan // rates.shape[0])
    packed = jnp.concatenate([state, head_k, head_v, tail_k, tail_v], axis=0)
    first, second = packed[:, : chan // 2], packed[:, chan // 2 :]
    zero = place_ref[0] == 0
    own_ref[...] = jnp.where(zero, first, second)
    other_ref[...] = jnp.where(zero, second, first)


def half_column(place_ref, rates_ref):
    col = column(rates_ref[...])
    middle = col.shape[0] // 2
    return jnp.where(place_ref[0] == 0, col[:middle], col[middle:])


def joined(tail_k, head_k, tail_v, head_v):
    return ((tail_k + head_k) * (tail_v + head_v)).astype(BF16).astype(F32)


def chip_kernel(place_ref, own_ref, got_ref, rates_ref, first_ref, spread_ref, *, hop, reach, per):
    zero = place_ref[0] == 0
    own, got = own_ref[...], got_ref[...]
    first = jnp.where(zero, own, got)
    second = jnp.where(zero, got, own)
    modes, width = first_ref.shape
    rate = by_channel(half_column(place_ref, rates_ref), modes, per, width)

    def part(value, k):
        return value[modes + k * HALO : modes + (k + 1) * HALO]

    seam = joined(part(first, 2), part(second, 0), part(first, 3), part(second, 1))
    chip = jnp.exp(-rate * hop) * first[:modes] + second[:modes]
    for s in range(reach):
        chip += jnp.exp(-rate * (hop - 1.0 - s)) * seam[s : s + 1]
    first_ref[...] = first[:modes]
    pieces = [chip] + [part(first, k)[:reach] for k in (0, 1)] + [part(second, k)[:reach] for k in (2, 3)]
    packed = jnp.concatenate(pieces, axis=0).astype(BF16)
    spread_ref[...] = jnp.broadcast_to(packed[None], spread_ref.shape)


def query_kernel(
    after_ref, hidden_hbm, gain_ref, w_hbm, taps_ref, inv_ref, edge_ref,
    query_ref, head_ref, tail_ref, hidden, near, total, ext, sems,
):
    rows, _ = hidden.shape
    chan = query_ref.shape[1]
    lines = copies(hidden_hbm, hidden, 1, 8, sems.at[0])
    weights = copies(w_hbm.at[:, pl.ds(0, chan)], near, 0, 8, sems.at[1])
    for line, weight in zip(lines, weights):
        line.start()
        weight.start()
    for line in lines:
        line.wait()

    def store(here, value):
        ext[HALO + here.start : HALO + here.stop, :] = value.astype(F32)

    ext[0:HALO, :] = jnp.zeros((HALO, chan), F32)
    multiply(hidden, inv_ref, gain_ref, near, total, weights, store)
    query_ref[...] = feature(taps_ref, ext, rows, 0, chan, 0)
    head_ref[:, :chan] = ext[HALO : 2 * HALO, :]
    head_ref[:, chan:] = edge_ref[0:HALO, :]
    tail = jnp.concatenate([ext[rows : rows + HALO, :], edge_ref[HALO:, :]], axis=1)
    tail_ref[...] = tail.astype(BF16)


def local_kernel(
    after_ref, prod_ref, skip_ref, rates_ref, residues_ref, rrow_ref, wrow_ref,
    base_ref, high_ref, low_ref,
):
    rows, chan = prod_ref.shape
    groups, modes = rates_ref.shape
    times = spot(0, rows).astype(F32) + 1.0
    high, low = split(wrow_ref[...] * jnp.exp(-rrow_ref[...] * times))
    high_ref[...] = high
    low_ref[...] = low
    rcol = column(rates_ref[...])
    wcol = column(residues_ref[...]) * jnp.sqrt(2.0 * rcol)
    block = 128
    blocks = rows // block
    span = (blocks + 1) * block
    per = chan // groups
    top = (blocks - 1) * block
    spots = spot(1, span)
    lags = jnp.where(spots <= top, top - spots, top + span - spots)
    used = (spots <= top) | (spots > blocks * block)
    terms = wcol * jnp.exp(-rcol * lags.astype(F32))
    terms = jnp.where(used, terms, 0.0)
    for g in range(groups):
        filt = jnp.sum(terms[g * modes : (g + 1) * modes, :], axis=0, keepdims=True)
        wide = jnp.broadcast_to(filt, (block, span))
        strip = pltpu.roll(wide, 0, 1, stride=1, stride_axis=0)[:, : blocks * block].astype(BF16)
        cols = slice(g * per, (g + 1) * per)
        mine = prod_ref[:, cols]
        for i in range(blocks):
            conv = dot(strip[:, (blocks - 1 - i) * block :], mine[: (i + 1) * block])
            here = slice(i * block, (i + 1) * block)
            base_ref[here, cols] = conv + skip_ref[:, cols] * mine[here].astype(F32)


def prefix_kernel(
    place_ref, all_ref, rates_ref, first_ref, after_ref, keep_ref, send_ref, seams, *, hop, reach, per
):
    count = all_ref.shape[0]
    modes, width = keep_ref.shape
    chip, zero = place_ref[1], place_ref[0] == 0
    col = half_column(place_ref, rates_ref)
    rate = by_channel(col, modes, per, width)
    fall = jnp.exp(-rate * (2.0 * hop))
    wide = all_ref[...].astype(F32)

    def part(k):
        return wide[:, modes + k * reach : modes + (k + 1) * reach, :]

    def before(k):
        value = part(k)
        return jnp.concatenate([jnp.zeros_like(value[:1]), value[:-1]], axis=0)

    seams[...] = jnp.zeros_like(seams)
    seams[:, 0:reach, :] = joined(before(2), part(0), before(3), part(1))
    total = jnp.zeros((modes, width), F32)
    for j in range(count):
        total = jnp.where(j < chip, fall * total + wide[j, :modes, :], total)
    index = spot(1, count * HALO)
    place, step = index // HALO, lax.rem(index, HALO)
    lag = 2.0 * hop * (chip - 1 - place).astype(F32) + (2.0 * hop - 1.0) - step.astype(F32)
    fade = jnp.where(place < chip, jnp.exp(-col * jnp.maximum(lag, 0.0)), 0.0)
    high, low = split(fade)
    products = seams[...].reshape(count * HALO, width).astype(BF16)
    total += fold(dot(high, products) + dot(low, products), modes, per)
    following = jnp.exp(-rate * hop) * total + first_ref[...]
    seam = seams[chip]
    for s in range(reach):
        following += jnp.exp(-rate * (hop - 1.0 - s)) * seam[s : s + 1, :]
    keep_ref[...] = jnp.where(zero, total, following)
    send_ref[...] = jnp.where(zero, following, total)


def mix_kernel(
    place_ref, query_ref, base_ref, keep_ref, back_ref, high_ref, low_ref, head_ref, halo_ref,
    taps_ref, skip_ref, rates_ref, residues_ref, w_hbm,
    out_hbm, w_ref, staged, gated, ext, shift, sums, sems,
):
    steps = sems.shape[1]
    weights = copies(w_hbm, w_ref, 1, steps, sems.at[0])
    for copy in weights:
        copy.start()
    rows, chan = query_ref.shape
    groups, modes = rates_ref.shape
    per = chan // groups
    reach = taps_ref.shape[0] - 1
    ext[0:HALO, :] = halo_ref[...].astype(F32)
    ext[HALO:, :] = head_ref[...]
    query, key, value = [feature(taps_ref, ext, HALO, n * chan, chan, n * chan) for n in range(3)]
    product = jnp.where(spot(0, HALO) < reach, key * value, 0.0).astype(BF16).astype(F32)
    shift[0:HALO, :] = product
    shift[HALO:, :] = jnp.zeros((HALO, chan), F32)
    rcol = column(rates_ref[...])
    wcol = column(residues_ref[...]) * jnp.sqrt(2.0 * rcol)
    rate = by_channel(rcol, modes, per, chan)
    weight = by_channel(wcol, modes, per, chan)

    zero = place_ref[0] == 0
    keep, back = keep_ref[...], back_ref[...]
    state = jnp.concatenate([jnp.where(zero, keep, back), jnp.where(zero, back, keep)], axis=1)
    for s in range(reach):
        state += jnp.exp(rate * (s + 1.0)) * product[s : s + 1, :]
    owner = spot(1, chan) // per
    spread = jnp.concatenate([jnp.where(owner == g, state, 0.0) for g in range(groups)], axis=0)
    high, low = split(spread)
    rise = high_ref[...]
    sums[...] = base_ref[...] + (dot(rise, high) + dot(low_ref[...], high) + dot(rise, low))
    start = sums[0:HALO, :] + skip_ref[...] * product
    for ahead in range(1, reach):
        above = jnp.sum(weight * jnp.exp(rate * float(ahead)), axis=0, keepdims=True)
        start -= above * shift[ahead : ahead + HALO, :]
    sums[...] = query_ref[...] * sums[...]
    sums[0:HALO, :] = query * start
    gated[...] = sums[...].astype(BF16)

    block = w_ref.shape[1] // steps
    sent = copies(staged, out_hbm, 1, steps, sems.at[1])
    for k in range(steps):
        cols = slice(k * block, (k + 1) * block)
        weights[k].wait()
        staged[:, cols] = dot(gated[...], w_ref[:, cols]).astype(BF16)
        sent[k].start()
    for copy in sent:
        copy.wait()


VMEM = pl.BlockSpec(memory_space=pltpu.VMEM)
SMEM = pl.BlockSpec(memory_space=pltpu.SMEM)
ANY = pl.BlockSpec(memory_space=pl.ANY)


def call(kernel, name, specs, outs, scratch=(), limit=40, flops=0, size=0, out_specs=None):
    return pl.pallas_call(
        kernel,
        in_specs=specs,
        out_specs=out_specs or [VMEM] * len(outs),
        out_shape=outs,
        scratch_shapes=list(scratch),
        compiler_params=pltpu.CompilerParams(vmem_limit_bytes=limit * MIB),
        cost_estimate=pl.CostEstimate(flops=flops, bytes_accessed=size, transcendentals=0),
        name=name,
    )


def in_hbm(value):
    return pltpu.with_memory_space_constraint(value, pltpu.HBM)


def on_device(hidden, norm_gain, w_in, w_short, residues, rates, skip, w_out):
    rows, width = hidden.shape
    columns = w_in.shape[1]
    chan = columns // 3
    half = chan // 2
    groups, modes = rates.shape
    per = chan // groups
    reach = w_short.shape[1] - 1
    devices = lax.axis_size("tm")
    here = lax.axis_index("tm")
    place = jnp.stack([here % 2, here // 2]).astype(jnp.int32)
    gain = norm_gain[None, :]
    taps = w_short.T
    skips = skip[None, :]
    vmem, sem = pltpu.VMEM, pltpu.SemaphoreType.DMA

    product, inv, edges, own, other = call(
        state_kernel,
        "state",
        [SMEM] + [ANY] * 5,
        [
            vmem((rows, chan), BF16),
            vmem((rows, 128), F32),
            vmem((2 * HALO, 2 * chan), F32),
            vmem((modes + 4 * HALO, half), F32),
            vmem((modes + 4 * HALO, half), F32),
        ],
        [
            vmem((rows, width), BF16),
            vmem((width, 2 * chan), BF16),
            vmem((1, width), F32),
            vmem((reach + 1, columns), F32),
            vmem((groups, modes), F32),
            vmem((rows, 2 * chan), F32),
            vmem((HALO + rows, 2 * chan), F32),
            vmem((2 * HALO, 2 * chan), F32),
            sem((3, 8)),
        ],
        flops=4 * rows * width * chan,
        size=2 * width * (rows + 2 * chan),
    )(place, in_hbm(hidden), in_hbm(gain), in_hbm(w_in), in_hbm(taps), in_hbm(rates))

    pairs = [(i, i ^ 1) for i in range(devices)]
    got = lax.ppermute(other, "tm", pairs)
    first, spread = call(
        functools.partial(chip_kernel, hop=float(rows), reach=reach, per=per),
        "chip",
        [SMEM] + [VMEM] * 3,
        [
            vmem((modes, half), F32),
            jax.ShapeDtypeStruct((devices // 2, modes + 4 * reach, half), BF16),
        ],
    )(place, own, got, rates)
    members = [list(range(c, devices, 2)) for c in range(2)]
    gathered = lax.all_to_all(spread, "tm", 0, 0, tiled=True, axis_index_groups=members)

    query, head, tail = call(
        query_kernel,
        "query",
        [VMEM, ANY, VMEM, ANY] + [VMEM] * 3,
        [vmem((rows, chan), F32), vmem((HALO, columns), F32), vmem((HALO, columns), BF16)],
        [
            vmem((rows, width), BF16),
            vmem((width, chan), BF16),
            vmem((rows, chan), F32),
            vmem((HALO + rows, chan), F32),
            sem((2, 8)),
        ],
        flops=2 * rows * width * chan,
        size=2 * width * (rows + chan),
    )(first, in_hbm(hidden), gain, in_hbm(w_in), taps, inv, edges)
    halo = lax.ppermute(tail, "tm", [(i, i + 1) for i in range(devices - 1)])

    weights = residues * jnp.sqrt(2.0 * rates)
    base, high, low = call(
        local_kernel,
        "local",
        [VMEM] * 7,
        [
            vmem((rows, chan), F32),
            vmem((rows, groups * modes), BF16),
            vmem((rows, groups * modes), BF16),
        ],
        flops=2 * rows * rows * chan,
        size=6 * rows * chan,
    )(tail, product, skips, rates, residues, rates.reshape(1, -1), weights.reshape(1, -1))

    keep, send = call(
        functools.partial(prefix_kernel, hop=float(rows), reach=reach, per=per),
        "prefix",
        [SMEM] + [VMEM] * 4,
        [vmem((modes, half), F32)] * 2,
        [vmem((devices // 2, HALO, half), F32)],
    )(place, gathered, rates, first, low)
    back = lax.ppermute(send, "tm", pairs)

    return call(
        mix_kernel,
        "mix",
        [SMEM] + [VMEM] * 12 + [ANY],
        jax.ShapeDtypeStruct((rows, w_out.shape[1]), BF16),
        [
            vmem(w_out.shape, BF16),
            vmem((rows, w_out.shape[1]), BF16),
            vmem((rows, chan), BF16),
            vmem((2 * HALO, columns), F32),
            vmem((2 * HALO, chan), F32),
            vmem((rows, chan), F32),
            sem((2, 8)),
        ],
        out_specs=ANY,
    )(
        place, query, base, keep, back, high, low, head, halo, taps, skips, rates, residues,
        in_hbm(w_out),
    )


def solution(mesh):
    return jax.shard_map(
        on_device,
        mesh=mesh,
        in_specs=(P("tm", None), P(), P(), P(), P(), P(), P(), P()),
        out_specs=P("tm", None),
        check_vma=False,
    )
```

```python
import functools

import jax
import jax.numpy as jnp
from jax import lax
from jax.experimental import pallas as pl
from jax.experimental.pallas import tpu as pltpu
from jax.sharding import PartitionSpec as P

F32 = jnp.float32
BF16 = jnp.bfloat16
HALO = 8
MIB = 1 << 20


def split(value):
    high = value.astype(BF16)
    return high, (value - high.astype(F32)).astype(BF16)


def dot(left, right):
    return jnp.dot(left, right, preferred_element_type=F32)


def spot(axis, count):
    shape = (1, count) if axis else (count, 1)
    return lax.broadcasted_iota(jnp.int32, shape, axis)


def copies(source, target, axis, count, sems):
    size = source.shape[axis] // count
    made = []
    for k in range(count):
        part = pl.ds(k * size, size)
        index = (part, slice(None)) if axis == 0 else (slice(None), part)
        made.append(pltpu.make_async_copy(source.at[index], target.at[index], sems.at[k]))
    return made


def column(table):
    groups, modes = table.shape
    rows = jnp.concatenate(
        [jnp.broadcast_to(table[g : g + 1, :], (modes, modes)) for g in range(groups)], axis=0
    )
    mine = spot(1, modes) == lax.rem(spot(0, groups * modes), modes)
    return jnp.sum(jnp.where(mine, rows, 0.0), axis=1, keepdims=True)


def fold(stacked, modes, per):
    width = stacked.shape[1]
    owner = spot(1, width) // per
    total = jnp.zeros((modes, width), F32)
    for g in range(stacked.shape[0] // modes):
        total = jnp.where(owner == g, stacked[g * modes : (g + 1) * modes, :], total)
    return total


def by_channel(col, modes, per, width):
    return fold(jnp.broadcast_to(col, (col.shape[0], width)), modes, per)


def feature(taps, ext, here, first, width, at=0):
    cols = slice(at, at + width)
    wide = slice(first, first + width)
    total = taps[0:1, wide] * ext[HALO + here.start : HALO + here.stop, cols]
    for k in range(1, taps.shape[0]):
        near = ext[HALO + here.start - k : HALO + here.stop - k, cols]
        total = total + taps[k : k + 1, wide] * near
    return total


EDGE = slice(0, HALO)


def multiply(hidden, inv, gain, near, total, weights, store, lines=(), late=1):
    rows = hidden.shape[0]
    count = len(weights)
    block = near.shape[0] // count
    part = rows // 3
    parts = [slice(first, first + part) for first in range(0, rows, part)]

    def made(here, k):
        cols = slice(k * block, (k + 1) * block)
        scale = jnp.concatenate([inv[here, :]] * (block // 128), axis=1)
        normed = (hidden[here, cols].astype(F32) * scale * gain[:, cols]).astype(BF16)
        return dot(normed, near[cols, :])

    def arrive(k):
        for copy in lines[k : k + 1]:
            copy.wait()
        weights[k].wait()

    for k in range(count - late):
        arrive(k)
        for here in parts:
            if k == 0:
                total[here, :] = made(here, k)
            else:
                total[here, :] += made(here, k)
    for here in parts:
        value = total[here, :]
        for k in range(count - late, count):
            if here.start == 0:
                arrive(k)
            value += made(here, k)
        store(here, value.astype(BF16))


def state_kernel(
    place_ref, hidden_hbm, gain_hbm, w_hbm, taps_hbm, rates_hbm,
    prod_ref, inv_ref, edge_ref, own_ref, other_ref,
    hidden, near, gain, taps, rates, total, ext, little, sems,
):
    rows, width = hidden.shape
    chan = prod_ref.shape[1]
    reach = taps.shape[0] - 1
    small = [
        pltpu.make_async_copy(source, target, sems.at[2, k])
        for k, (source, target) in enumerate(
            ((gain_hbm, gain), (taps_hbm, taps), (rates_hbm, rates))
        )
    ]
    lines = copies(hidden_hbm, hidden, 1, 8, sems.at[0])
    weights = copies(w_hbm.at[:, pl.ds(chan, 2 * chan)], near, 0, 8, sems.at[1])
    for copy in small + lines:
        copy.start()
    inv_ref[...] = jnp.zeros_like(inv_ref)
    ext[0:HALO, :] = jnp.zeros((HALO, 2 * chan), F32)
    for copy in small:
        copy.wait()
    modes = rates.shape[1]
    left = (rows - 1 - spot(1, rows)).astype(F32)
    high, low = split(jnp.exp(-column(rates[...]) * left))
    block = width // len(lines)
    for k, copy in enumerate(lines):
        copy.wait()
        weights[k].start()

        def add(i, _, k=k):
            cols = pl.ds(pl.multiple_of(k * block + i * 256, 256), 256)
            wide = hidden[:, cols].astype(F32)
            square = wide * wide
            inv_ref[...] += square[:, :128] + square[:, 128:]
            return 0

        lax.fori_loop(0, block // 256, add, 0)
    inv = lax.rsqrt(jnp.sum(inv_ref[...], axis=1, keepdims=True) / width + 1e-06)
    inv_ref[...] = jnp.broadcast_to(inv, inv_ref.shape)
    crossed, heads = [], []

    def store(here, value):
        ext[HALO + here.start : HALO + here.stop, :] = value.astype(F32)
        key = feature(taps, ext, here, chan, chan, 0)
        value = feature(taps, ext, here, 2 * chan, chan, chan)
        product = key * value
        if here.start == 0:
            early = spot(0, HALO) < reach
            heads.extend(jnp.where(early, kind[0:HALO, :], 0.0) for kind in (key, value))
            product = jnp.where(spot(0, here.stop) >= reach, product, 0.0)
        product = product.astype(BF16)
        prod_ref[here, :] = product
        crossed.append(dot(high[:, here], product) + dot(low[:, here], product))

    multiply(hidden, inv_ref, gain, near, total, weights, store, late=4)

    edge_ref[0:HALO, :] = ext[HALO : 2 * HALO, :]
    edge_ref[HALO:, :] = ext[rows : rows + HALO, :]
    little[0:HALO, :] = ext[rows : rows + HALO, :]
    little[HALO:, :] = jnp.zeros((HALO, 2 * chan), F32)
    tail_k = feature(taps, little, EDGE, chan, chan, 0)
    tail_v = feature(taps, little, EDGE, 2 * chan, chan, chan)
    state = fold(sum(crossed[1:], crossed[0]), modes, chan // rates.shape[0])
    packed = jnp.concatenate([state] + heads + [tail_k, tail_v], axis=0)
    first, second = packed[:, : chan // 2], packed[:, chan // 2 :]
    zero = place_ref[0] == 0
    own_ref[...] = jnp.where(zero, first, second)
    other_ref[...] = jnp.where(zero, second, first)


def half_column(place_ref, rates_ref):
    col = column(rates_ref[...])
    middle = col.shape[0] // 2
    return jnp.where(place_ref[0] == 0, col[:middle], col[middle:])


def joined(tail_k, head_k, tail_v, head_v):
    return ((tail_k + head_k) * (tail_v + head_v)).astype(BF16).astype(F32)


def chip_kernel(place_ref, own_ref, got_ref, rates_ref, first_ref, spread_ref, *, hop, reach, per):
    zero = place_ref[0] == 0
    own, got = own_ref[...], got_ref[...]
    first = jnp.where(zero, own, got)
    second = jnp.where(zero, got, own)
    modes, width = first_ref.shape
    rate = by_channel(half_column(place_ref, rates_ref), modes, per, width)

    def part(value, k):
        return value[modes + k * HALO : modes + (k + 1) * HALO]

    seam = joined(part(first, 2), part(second, 0), part(first, 3), part(second, 1))
    chip = jnp.exp(-rate * hop) * first[:modes] + second[:modes]
    for s in range(reach):
        chip += jnp.exp(-rate * (hop - 1.0 - s)) * seam[s : s + 1]
    first_ref[...] = first[:modes]
    pieces = [chip] + [part(first, k)[:reach] for k in (0, 1)] + [part(second, k)[:reach] for k in (2, 3)]
    packed = jnp.concatenate(pieces, axis=0).astype(BF16)
    spread_ref[...] = jnp.broadcast_to(packed[None], spread_ref.shape)


def query_kernel(
    after_ref, hidden_hbm, gain_ref, w_hbm, taps_ref, inv_ref, edge_ref,
    query_ref, head_ref, tail_ref, hidden, near, total, ext, sems,
):
    rows, _ = hidden.shape
    chan = query_ref.shape[1]
    lines = copies(hidden_hbm, hidden, 1, 8, sems.at[0])
    weights = copies(w_hbm.at[:, pl.ds(0, chan)], near, 0, 8, sems.at[1])
    for line, weight in zip(lines, weights):
        line.start()
        weight.start()

    def store(here, value):
        ext[HALO + here.start : HALO + here.stop, :] = value.astype(F32)
        query_ref[here, :] = feature(taps_ref, ext, here, 0, chan, 0)

    ext[0:HALO, :] = jnp.zeros((HALO, chan), F32)
    multiply(hidden, inv_ref, gain_ref, near, total, weights, store, lines)
    head_ref[:, :chan] = ext[HALO : 2 * HALO, :]
    head_ref[:, chan:] = edge_ref[0:HALO, :]
    tail = jnp.concatenate([ext[rows : rows + HALO, :], edge_ref[HALO:, :]], axis=1)
    tail_ref[...] = tail.astype(BF16)


def local_kernel(
    after_ref, prod_ref, skip_ref, rates_ref, residues_ref, rrow_ref, wrow_ref, w_hbm,
    base_ref, high_ref, low_ref, near_ref, sem,
):
    fetch = pltpu.make_async_copy(w_hbm.at[:, pl.ds(0, near_ref.shape[1])], near_ref, sem)
    fetch.start()
    rows, chan = prod_ref.shape
    groups, modes = rates_ref.shape
    times = spot(0, rows).astype(F32) + 1.0
    high, low = split(wrow_ref[...] * jnp.exp(-rrow_ref[...] * times))
    high_ref[...] = high
    low_ref[...] = low
    rcol = column(rates_ref[...])
    wcol = column(residues_ref[...]) * jnp.sqrt(2.0 * rcol)
    block = 128
    blocks = rows // block
    span = (blocks + 1) * block
    per = chan // groups
    top = (blocks - 1) * block
    spots = spot(1, span)
    lags = jnp.where(spots <= top, top - spots, top + span - spots)
    used = (spots <= top) | (spots > blocks * block)
    terms = wcol * jnp.exp(-rcol * lags.astype(F32))
    terms = jnp.where(used, terms, 0.0)
    for g in range(groups):
        filt = jnp.sum(terms[g * modes : (g + 1) * modes, :], axis=0, keepdims=True)
        wide = jnp.broadcast_to(filt, (block, span))
        strip = pltpu.roll(wide, 0, 1, stride=1, stride_axis=0)[:, : blocks * block].astype(BF16)
        cols = slice(g * per, (g + 1) * per)
        mine = prod_ref[:, cols]
        for i in range(blocks):
            conv = dot(strip[:, (blocks - 1 - i) * block :], mine[: (i + 1) * block])
            here = slice(i * block, (i + 1) * block)
            base_ref[here, cols] = conv + skip_ref[:, cols] * mine[here].astype(F32)
    fetch.wait()


def prefix_kernel(
    place_ref, all_ref, rates_ref, first_ref, after_ref, keep_ref, send_ref, seams, *, hop, reach, per
):
    count = all_ref.shape[0]
    modes, width = keep_ref.shape
    chip, zero = place_ref[1], place_ref[0] == 0
    col = half_column(place_ref, rates_ref)
    rate = by_channel(col, modes, per, width)
    fall = jnp.exp(-rate * (2.0 * hop))
    wide = all_ref[...].astype(F32)

    def part(k):
        return wide[:, modes + k * reach : modes + (k + 1) * reach, :]

    def before(k):
        value = part(k)
        return jnp.concatenate([jnp.zeros_like(value[:1]), value[:-1]], axis=0)

    seams[...] = jnp.zeros_like(seams)
    seams[:, 0:reach, :] = joined(before(2), part(0), before(3), part(1))
    total = jnp.zeros((modes, width), F32)
    for j in range(count):
        total = jnp.where(j < chip, fall * total + wide[j, :modes, :], total)
    index = spot(1, count * HALO)
    place, step = index // HALO, lax.rem(index, HALO)
    lag = 2.0 * hop * (chip - 1 - place).astype(F32) + (2.0 * hop - 1.0) - step.astype(F32)
    fade = jnp.where(place < chip, jnp.exp(-col * jnp.maximum(lag, 0.0)), 0.0)
    high, low = split(fade)
    products = seams[...].reshape(count * HALO, width).astype(BF16)
    total += fold(dot(high, products) + dot(low, products), modes, per)
    following = jnp.exp(-rate * hop) * total + first_ref[...]
    seam = seams[chip]
    for s in range(reach):
        following += jnp.exp(-rate * (hop - 1.0 - s)) * seam[s : s + 1, :]
    keep_ref[...] = jnp.where(zero, total, following)
    send_ref[...] = jnp.where(zero, following, total)


def mix_kernel(
    place_ref, query_ref, base_ref, keep_ref, back_ref, high_ref, low_ref, head_ref, halo_ref,
    taps_ref, skip_ref, rates_ref, residues_ref, near_ref, w_hbm,
    out_hbm, w_ref, staged, gated, ext, shift, sums, sems,
):
    steps = sems.shape[1]
    kept = near_ref.shape[1]
    block = out_hbm.shape[1] // steps
    rest = w_ref.shape[1]
    weights = copies(w_hbm.at[:, pl.ds(kept, rest)], w_ref, 1, rest // block, sems.at[0])
    for copy in weights:
        copy.start()
    rows, chan = query_ref.shape
    groups, modes = rates_ref.shape
    per = chan // groups
    reach = taps_ref.shape[0] - 1
    ext[0:HALO, :] = halo_ref[...].astype(F32)
    ext[HALO:, :] = head_ref[...]
    query, key, value = [feature(taps_ref, ext, EDGE, n * chan, chan, n * chan) for n in range(3)]
    product = jnp.where(spot(0, HALO) < reach, key * value, 0.0).astype(BF16).astype(F32)
    shift[0:HALO, :] = product
    shift[HALO:, :] = jnp.zeros((HALO, chan), F32)
    rcol = column(rates_ref[...])
    wcol = column(residues_ref[...]) * jnp.sqrt(2.0 * rcol)
    rate = by_channel(rcol, modes, per, chan)
    weight = by_channel(wcol, modes, per, chan)

    zero = place_ref[0] == 0
    keep, back = keep_ref[...], back_ref[...]
    state = jnp.concatenate([jnp.where(zero, keep, back), jnp.where(zero, back, keep)], axis=1)
    for s in range(reach):
        state += jnp.exp(rate * (s + 1.0)) * product[s : s + 1, :]
    owner = spot(1, chan) // per
    spread = jnp.concatenate([jnp.where(owner == g, state, 0.0) for g in range(groups)], axis=0)
    high, low = split(spread)
    rise = high_ref[...]
    sums[...] = base_ref[...] + (dot(rise, high) + dot(low_ref[...], high) + dot(rise, low))
    start = sums[0:HALO, :] + skip_ref[...] * product
    for ahead in range(1, reach):
        above = jnp.sum(weight * jnp.exp(rate * float(ahead)), axis=0, keepdims=True)
        start -= above * shift[ahead : ahead + HALO, :]
    sums[...] = query_ref[...] * sums[...]
    sums[0:HALO, :] = query * start
    gated[...] = sums[...].astype(BF16)

    sent = copies(staged, out_hbm, 1, steps, sems.at[1])
    for k in range(steps):
        source, first = near_ref, k * block
        if first >= kept:
            source, first = w_ref, first - kept
            weights[first // block].wait()
        made = dot(gated[...], source[:, first : first + block])
        staged[:, k * block : (k + 1) * block] = made.astype(BF16)
        sent[k].start()
    for copy in sent:
        copy.wait()


VMEM = pl.BlockSpec(memory_space=pltpu.VMEM)
SMEM = pl.BlockSpec(memory_space=pltpu.SMEM)
ANY = pl.BlockSpec(memory_space=pl.ANY)


def call(kernel, name, specs, outs, scratch=(), limit=40, flops=0, size=0, out_specs=None):
    return pl.pallas_call(
        kernel,
        in_specs=specs,
        out_specs=out_specs or [VMEM] * len(outs),
        out_shape=outs,
        scratch_shapes=list(scratch),
        compiler_params=pltpu.CompilerParams(vmem_limit_bytes=limit * MIB),
        cost_estimate=pl.CostEstimate(flops=flops, bytes_accessed=size, transcendentals=0),
        name=name,
    )


def in_hbm(value):
    return pltpu.with_memory_space_constraint(value, pltpu.HBM)


def on_device(hidden, norm_gain, w_in, w_short, residues, rates, skip, w_out):
    rows, width = hidden.shape
    columns = w_in.shape[1]
    chan = columns // 3
    half = chan // 2
    groups, modes = rates.shape
    per = chan // groups
    reach = w_short.shape[1] - 1
    devices = lax.axis_size("tm")
    here = lax.axis_index("tm")
    place = jnp.stack([here % 2, here // 2]).astype(jnp.int32)
    gain = norm_gain[None, :]
    taps = w_short.T
    skips = skip[None, :]
    vmem, sem = pltpu.VMEM, pltpu.SemaphoreType.DMA

    product, inv, edges, own, other = call(
        state_kernel,
        "state",
        [SMEM] + [ANY] * 5,
        [
            vmem((rows, chan), BF16),
            vmem((rows, 128), F32),
            vmem((2 * HALO, 2 * chan), F32),
            vmem((modes + 4 * HALO, half), F32),
            vmem((modes + 4 * HALO, half), F32),
        ],
        [
            vmem((rows, width), BF16),
            vmem((width, 2 * chan), BF16),
            vmem((1, width), F32),
            vmem((reach + 1, columns), F32),
            vmem((groups, modes), F32),
            vmem((rows, 2 * chan), F32),
            vmem((HALO + rows, 2 * chan), F32),
            vmem((2 * HALO, 2 * chan), F32),
            sem((3, 8)),
        ],
        flops=4 * rows * width * chan,
        size=2 * width * (rows + 2 * chan),
    )(place, in_hbm(hidden), in_hbm(gain), in_hbm(w_in), in_hbm(taps), in_hbm(rates))

    pairs = [(i, i ^ 1) for i in range(devices)]
    got = lax.ppermute(other, "tm", pairs)
    first, spread = call(
        functools.partial(chip_kernel, hop=float(rows), reach=reach, per=per),
        "chip",
        [SMEM] + [VMEM] * 3,
        [
            vmem((modes, half), F32),
            jax.ShapeDtypeStruct((devices // 2, modes + 4 * reach, half), BF16),
        ],
    )(place, own, got, rates)
    members = [list(range(c, devices, 2)) for c in range(2)]
    gathered = lax.all_to_all(spread, "tm", 0, 0, tiled=True, axis_index_groups=members)

    query, head, tail = call(
        query_kernel,
        "query",
        [VMEM, ANY, VMEM, ANY] + [VMEM] * 3,
        [vmem((rows, chan), F32), vmem((HALO, columns), F32), vmem((HALO, columns), BF16)],
        [
            vmem((rows, width), BF16),
            vmem((width, chan), BF16),
            vmem((rows, chan), F32),
            vmem((HALO + rows, chan), F32),
            sem((2, 8)),
        ],
        flops=2 * rows * width * chan,
        size=2 * width * (rows + chan),
    )(first, in_hbm(hidden), gain, in_hbm(w_in), taps, inv, edges)
    halo = lax.ppermute(tail, "tm", [(i, i + 1) for i in range(devices - 1)])

    weights = residues * jnp.sqrt(2.0 * rates)
    kept = w_out.shape[1] * 3 // 8
    base, high, low, w_near = call(
        local_kernel,
        "local",
        [VMEM] * 7 + [ANY],
        [
            vmem((rows, chan), F32),
            vmem((rows, groups * modes), BF16),
            vmem((rows, groups * modes), BF16),
            vmem((chan, kept), BF16),
        ],
        [sem],
        flops=2 * rows * rows * chan,
        size=6 * rows * chan,
    )(
        tail, product, skips, rates, residues, rates.reshape(1, -1), weights.reshape(1, -1),
        in_hbm(w_out),
    )

    keep, send = call(
        functools.partial(prefix_kernel, hop=float(rows), reach=reach, per=per),
        "prefix",
        [SMEM] + [VMEM] * 4,
        [vmem((modes, half), F32)] * 2,
        [vmem((devices // 2, HALO, half), F32)],
    )(place, gathered, rates, first, low)
    back = lax.ppermute(send, "tm", pairs)

    return call(
        mix_kernel,
        "mix",
        [SMEM] + [VMEM] * 13 + [ANY],
        jax.ShapeDtypeStruct((rows, w_out.shape[1]), BF16),
        [
            vmem((chan, w_out.shape[1] - kept), BF16),
            vmem((rows, w_out.shape[1]), BF16),
            vmem((rows, chan), BF16),
            vmem((2 * HALO, columns), F32),
            vmem((2 * HALO, chan), F32),
            vmem((rows, chan), F32),
            sem((2, 8)),
        ],
        out_specs=ANY,
    )(
        place, query, base, keep, back, high, low, head, halo, taps, skips, rates, residues,
        w_near, in_hbm(w_out),
    )


def solution(mesh):
    return jax.shard_map(
        on_device,
        mesh=mesh,
        in_specs=(P("tm", None), P(), P(), P(), P(), P(), P(), P()),
        out_specs=P("tm", None),
        check_vma=False,
    )
```

```python
import functools

import jax
import jax.numpy as jnp
from jax import lax
from jax.experimental import pallas as pl
from jax.experimental.pallas import tpu as pltpu
from jax.sharding import PartitionSpec as P

F32 = jnp.float32
BF16 = jnp.bfloat16
HALO = 8
MIB = 1 << 20


def split(value):
    high = value.astype(BF16)
    return high, (value - high.astype(F32)).astype(BF16)


def dot(left, right):
    return jnp.dot(left, right, preferred_element_type=F32)


def spot(axis, count):
    shape = (1, count) if axis else (count, 1)
    return lax.broadcasted_iota(jnp.int32, shape, axis)


def copies(source, target, axis, count, sems):
    size = source.shape[axis] // count
    made = []
    for k in range(count):
        part = pl.ds(k * size, size)
        index = (part, slice(None)) if axis == 0 else (slice(None), part)
        made.append(pltpu.make_async_copy(source.at[index], target.at[index], sems.at[k]))
    return made


def column(table):
    groups, modes = table.shape
    rows = jnp.concatenate(
        [jnp.broadcast_to(table[g : g + 1, :], (modes, modes)) for g in range(groups)], axis=0
    )
    mine = spot(1, modes) == lax.rem(spot(0, groups * modes), modes)
    return jnp.sum(jnp.where(mine, rows, 0.0), axis=1, keepdims=True)


def fold(stacked, modes, per):
    width = stacked.shape[1]
    owner = spot(1, width) // per
    total = jnp.zeros((modes, width), F32)
    for g in range(stacked.shape[0] // modes):
        total = jnp.where(owner == g, stacked[g * modes : (g + 1) * modes, :], total)
    return total


def by_channel(col, modes, per, width):
    return fold(jnp.broadcast_to(col, (col.shape[0], width)), modes, per)


def feature(taps, ext, here, first, width, at=0):
    cols = slice(at, at + width)
    wide = slice(first, first + width)
    total = taps[0:1, wide] * ext[HALO + here.start : HALO + here.stop, cols]
    for k in range(1, taps.shape[0]):
        near = ext[HALO + here.start - k : HALO + here.stop - k, cols]
        total = total + taps[k : k + 1, wide] * near
    return total


EDGE = slice(0, HALO)


def multiply(hidden, inv, gain, near, total, weights, store, lines=(), late=1):
    rows = hidden.shape[0]
    count = len(weights)
    block = near.shape[0] // count
    part = rows // 3
    parts = [slice(first, first + part) for first in range(0, rows, part)]

    def made(here, k):
        cols = slice(k * block, (k + 1) * block)
        scale = jnp.concatenate([inv[here, :]] * (block // 128), axis=1)
        normed = (hidden[here, cols].astype(F32) * scale * gain[:, cols]).astype(BF16)
        return dot(normed, near[cols, :])

    def arrive(k):
        for copy in lines[k : k + 1]:
            copy.wait()
        weights[k].wait()

    for k in range(count - late):
        arrive(k)
        for here in parts:
            if k == 0:
                total[here, :] = made(here, k)
            else:
                total[here, :] += made(here, k)
    for here in parts:
        value = total[here, :]
        for k in range(count - late, count):
            if here.start == 0:
                arrive(k)
            value += made(here, k)
        store(here, value.astype(BF16))


def state_kernel(
    place_ref, hidden_hbm, gain_hbm, w_hbm, taps_hbm, rates_hbm,
    prod_ref, inv_ref, edge_ref, own_ref, other_ref,
    hidden, near, gain, taps, rates, total, ext, little, sems,
):
    rows, width = hidden.shape
    chan = prod_ref.shape[1]
    reach = taps.shape[0] - 1
    small = [
        pltpu.make_async_copy(source, target, sems.at[2, k])
        for k, (source, target) in enumerate(
            ((gain_hbm, gain), (taps_hbm, taps), (rates_hbm, rates))
        )
    ]
    lines = copies(hidden_hbm, hidden, 1, 8, sems.at[0])
    weights = copies(w_hbm.at[:, pl.ds(chan, 2 * chan)], near, 0, 8, sems.at[1])
    for copy in small + lines:
        copy.start()
    inv_ref[...] = jnp.zeros_like(inv_ref)
    ext[0:HALO, :] = jnp.zeros((HALO, 2 * chan), F32)
    for copy in small:
        copy.wait()
    modes = rates.shape[1]
    left = (rows - 1 - spot(1, rows)).astype(F32)
    high, low = split(jnp.exp(-column(rates[...]) * left))
    block = width // len(lines)
    for k, copy in enumerate(lines):
        copy.wait()
        weights[k].start()

        def add(i, _, k=k):
            cols = pl.ds(pl.multiple_of(k * block + i * 256, 256), 256)
            wide = hidden[:, cols].astype(F32)
            square = wide * wide
            inv_ref[...] += square[:, :128] + square[:, 128:]
            return 0

        lax.fori_loop(0, block // 256, add, 0)
    inv = lax.rsqrt(jnp.sum(inv_ref[...], axis=1, keepdims=True) / width + 1e-06)
    inv_ref[...] = jnp.broadcast_to(inv, inv_ref.shape)
    crossed, heads = [], []

    def store(here, value):
        ext[HALO + here.start : HALO + here.stop, :] = value.astype(F32)
        key = feature(taps, ext, here, chan, chan, 0)
        value = feature(taps, ext, here, 2 * chan, chan, chan)
        product = key * value
        if here.start == 0:
            early = spot(0, HALO) < reach
            heads.extend(jnp.where(early, kind[0:HALO, :], 0.0) for kind in (key, value))
            product = jnp.where(spot(0, here.stop) >= reach, product, 0.0)
        product = product.astype(BF16)
        prod_ref[here, :] = product
        crossed.append(dot(high[:, here], product) + dot(low[:, here], product))

    multiply(hidden, inv_ref, gain, near, total, weights, store, late=4)

    edge_ref[0:HALO, :] = ext[HALO : 2 * HALO, :]
    edge_ref[HALO:, :] = ext[rows : rows + HALO, :]
    little[0:HALO, :] = ext[rows : rows + HALO, :]
    little[HALO:, :] = jnp.zeros((HALO, 2 * chan), F32)
    tail_k = feature(taps, little, EDGE, chan, chan, 0)
    tail_v = feature(taps, little, EDGE, 2 * chan, chan, chan)
    state = fold(sum(crossed[1:], crossed[0]), modes, chan // rates.shape[0])
    packed = jnp.concatenate([state] + heads + [tail_k, tail_v], axis=0)
    first, second = packed[:, : chan // 2], packed[:, chan // 2 :]
    zero = place_ref[0] == 0
    own_ref[...] = jnp.where(zero, first, second)
    other_ref[...] = jnp.where(zero, second, first)


def half_column(place_ref, rates_ref):
    col = column(rates_ref[...])
    middle = col.shape[0] // 2
    return jnp.where(place_ref[0] == 0, col[:middle], col[middle:])


def joined(tail_k, head_k, tail_v, head_v):
    return ((tail_k + head_k) * (tail_v + head_v)).astype(BF16).astype(F32)


def part(value, modes, k):
    return value[modes + k * HALO : modes + (k + 1) * HALO]


def merge(left, right, rate, length):
    modes = rate.shape[0]
    seam = joined(*[part(v, modes, k) for v, k in ((left, 2), (right, 0), (left, 3), (right, 1))])
    state = jnp.exp(-rate * length) * left[:modes] + right[:modes] + entering(seam, rate, length)
    return jnp.concatenate(
        [state, left[modes : modes + 2 * HALO], right[modes + 2 * HALO :]], axis=0
    )


def entering(seam, rate, length):
    total = jnp.zeros(rate.shape, F32)
    for s in range(HALO - 2):
        total += jnp.exp(-rate * (length - 1.0 - s)) * seam[s : s + 1]
    return total


def chip_kernel(place_ref, own_ref, got_ref, rates_ref, first_ref, chip_ref, *, hop, per):
    zero = place_ref[0] == 0
    own, got = own_ref[...], got_ref[...]
    first = jnp.where(zero, own, got)
    second = jnp.where(zero, got, own)
    modes, width = first_ref.shape
    rate = by_channel(half_column(place_ref, rates_ref), modes, per, width)
    first_ref[...] = first[:modes]
    chip_ref[...] = merge(first, second, rate, hop)


def line_kernel(place_ref, own_ref, *refs, hop, reach, per, along):
    got_refs, (rates_ref, tail_ref, spread_ref, inner_ref, early_ref, sent_ref) = (
        refs[: along - 1], refs[along - 1 :]
    )
    sent_ref[...] = tail_ref[...]
    own = own_ref[...]
    modes = rates_ref.shape[1]
    rate = by_channel(half_column(place_ref, rates_ref), modes, per, own.shape[1])
    spot_x = place_ref[1]
    chips = []
    for j in range(along):
        chip = own
        for m in range(1, along):
            chip = jnp.where(spot_x == (j ^ m), got_refs[m - 1][...], chip)
        chips.append(chip)
    total = chips[0]
    before = jnp.zeros_like(total)
    for j in range(1, along):
        before = jnp.where(spot_x == j, total, before)
        total = merge(total, chips[j], rate, 2.0 * hop)
    inner_ref[...] = before
    early_ref[...] = own[modes : modes + 2 * HALO]
    pieces = [total[:modes]] + [part(total, modes, k)[:reach] for k in range(4)]
    packed = jnp.concatenate(pieces, axis=0).astype(BF16)
    spread_ref[...] = jnp.broadcast_to(packed[None], spread_ref.shape)


def query_kernel(
    after_ref, hidden_hbm, gain_ref, w_hbm, taps_ref, inv_ref, edge_ref,
    query_ref, head_ref, tail_ref, hidden, near, total, ext, sems,
):
    rows, _ = hidden.shape
    chan = query_ref.shape[1]
    lines = copies(hidden_hbm, hidden, 1, 8, sems.at[0])
    weights = copies(w_hbm.at[:, pl.ds(0, chan)], near, 0, 8, sems.at[1])
    for line, weight in zip(lines, weights):
        line.start()
        weight.start()

    def store(here, value):
        ext[HALO + here.start : HALO + here.stop, :] = value.astype(F32)
        query_ref[here, :] = feature(taps_ref, ext, here, 0, chan, 0)

    ext[0:HALO, :] = jnp.zeros((HALO, chan), F32)
    multiply(hidden, inv_ref, gain_ref, near, total, weights, store, lines)
    head_ref[:, :chan] = ext[HALO : 2 * HALO, :]
    head_ref[:, chan:] = edge_ref[0:HALO, :]
    tail = jnp.concatenate([ext[rows : rows + HALO, :], edge_ref[HALO:, :]], axis=1)
    tail_ref[...] = tail.astype(BF16)


def local_kernel(
    after_ref, prod_ref, skip_ref, rates_ref, residues_ref, rrow_ref, wrow_ref, w_hbm,
    base_ref, high_ref, low_ref, near_ref, sem,
):
    fetch = pltpu.make_async_copy(w_hbm.at[:, pl.ds(0, near_ref.shape[1])], near_ref, sem)
    fetch.start()
    rows, chan = prod_ref.shape
    groups, modes = rates_ref.shape
    times = spot(0, rows).astype(F32) + 1.0
    high, low = split(wrow_ref[...] * jnp.exp(-rrow_ref[...] * times))
    high_ref[...] = high
    low_ref[...] = low
    rcol = column(rates_ref[...])
    wcol = column(residues_ref[...]) * jnp.sqrt(2.0 * rcol)
    block = 128
    per = chan // groups
    places = [slice(first, first + block) for first in range(0, rows, block)]
    for here in places:
        base_ref[here, :] = skip_ref[...] * prod_ref[here, :].astype(F32)

    keep = spot(1, chan) // per == spot(0, groups * modes) // modes
    leave_high, leave_low = split(jnp.exp(-rcol * (block - 1 - spot(1, block)).astype(F32)))
    fall = jnp.exp(-rcol * float(block))
    state = jnp.zeros((groups * modes, chan), F32)
    for here, following in zip(places, places[1:]):
        mine = prod_ref[here, :]
        state = fall * state + (dot(leave_high, mine) + dot(leave_low, mine))
        near_high, near_low = split(jnp.where(keep, state, 0.0))
        rise = high[:block, :]
        base_ref[following, :] += (
            dot(rise, near_high) + dot(low[:block, :], near_high) + dot(rise, near_low)
        )

    span = 2 * block
    spots = spot(1, span)
    lags = jnp.where(spots == 0, 0, span - spots)
    terms = wcol * jnp.exp(-rcol * lags.astype(F32))
    terms = jnp.where((spots == 0) | (spots > block), terms, 0.0)
    for g in range(groups):
        filt = jnp.sum(terms[g * modes : (g + 1) * modes, :], axis=0, keepdims=True)
        wide = jnp.broadcast_to(filt, (block, span))
        square = pltpu.roll(wide, 0, 1, stride=1, stride_axis=0)[:, :block].astype(BF16)
        cols = slice(g * per, (g + 1) * per)
        for here in places:
            base_ref[here, cols] += dot(square, prod_ref[here, cols])
    fetch.wait()


def prefix_kernel(
    place_ref, all_ref, rates_ref, first_ref, inner_ref, early_ref, after_ref,
    keep_ref, send_ref, seams, tails, *, hop, reach, per, along,
):
    count = all_ref.shape[0]
    modes, width = keep_ref.shape
    zero, spot_x, line = place_ref[0] == 0, place_ref[1], place_ref[2]
    col = half_column(place_ref, rates_ref)
    rate = by_channel(col, modes, per, width)
    span = 2.0 * hop * along
    fall = jnp.exp(-rate * span)
    wide = all_ref[...].astype(F32)

    def piece(k):
        return wide[:, modes + k * reach : modes + (k + 1) * reach, :]

    def before(k):
        value = piece(k)
        return jnp.concatenate([jnp.zeros_like(value[:1]), value[:-1]], axis=0)

    seams[...] = jnp.zeros_like(seams)
    tails[...] = jnp.zeros_like(tails)
    tail_k, tail_v = before(2), before(3)
    tails[:, 0:reach, :] = tail_k
    tails[:, HALO : HALO + reach, :] = tail_v
    seams[:, 0:reach, :] = joined(tail_k, piece(0), tail_v, piece(1))
    total = jnp.zeros((modes, width), F32)
    for j in range(count):
        total = jnp.where(j < line, fall * total + wide[j, :modes, :], total)
    index = spot(1, count * HALO)
    place, step = index // HALO, lax.rem(index, HALO)
    lag = span * (line - 1 - place).astype(F32) + (span - 1.0) - step.astype(F32)
    fade = jnp.where(place < line, jnp.exp(-col * jnp.maximum(lag, 0.0)), 0.0)
    high, low = split(fade)
    products = seams[...].reshape(count * HALO, width).astype(BF16)
    total += fold(dot(high, products) + dot(low, products), modes, per)

    inner, early = inner_ref[...], early_ref[...]
    outer = tails[line]
    heads = [part(inner, modes, k) for k in (0, 1)]
    seam = joined(outer[:HALO], heads[0], outer[HALO:], heads[1])
    length = 2.0 * hop * spot_x.astype(F32)
    within = jnp.exp(-rate * length) * total + inner[:modes]
    for s in range(reach):
        within += jnp.exp(-rate * jnp.maximum(length - 1.0 - s, 0.0)) * seam[s : s + 1]
    starts = spot_x == 0
    total = jnp.where(starts, total, within)
    last_k = jnp.where(starts, outer[:HALO], part(inner, modes, 2))
    last_v = jnp.where(starts, outer[HALO:], part(inner, modes, 3))
    seam = joined(last_k, early[:HALO], last_v, early[HALO:])
    following = jnp.exp(-rate * hop) * total + first_ref[...] + entering(seam, rate, hop)
    keep_ref[...] = jnp.where(zero, total, following)
    send_ref[...] = jnp.where(zero, following, total)


def mix_kernel(
    place_ref, query_ref, base_ref, keep_ref, back_ref, high_ref, low_ref, head_ref, halo_ref,
    taps_ref, skip_ref, rates_ref, residues_ref, near_ref, w_hbm,
    out_hbm, w_ref, staged, gated, ext, shift, sums, sems,
):
    steps = sems.shape[1]
    kept = near_ref.shape[1]
    block = out_hbm.shape[1] // steps
    rest = w_ref.shape[1]
    weights = copies(w_hbm.at[:, pl.ds(kept, rest)], w_ref, 1, rest // block, sems.at[0])
    for copy in weights:
        copy.start()
    rows, chan = query_ref.shape
    groups, modes = rates_ref.shape
    per = chan // groups
    reach = taps_ref.shape[0] - 1
    ext[0:HALO, :] = halo_ref[...].astype(F32)
    ext[HALO:, :] = head_ref[...]
    query, key, value = [feature(taps_ref, ext, EDGE, n * chan, chan, n * chan) for n in range(3)]
    product = jnp.where(spot(0, HALO) < reach, key * value, 0.0).astype(BF16).astype(F32)
    shift[0:HALO, :] = product
    shift[HALO:, :] = jnp.zeros((HALO, chan), F32)
    rcol = column(rates_ref[...])
    wcol = column(residues_ref[...]) * jnp.sqrt(2.0 * rcol)
    rate = by_channel(rcol, modes, per, chan)
    weight = by_channel(wcol, modes, per, chan)

    zero = place_ref[0] == 0
    keep, back = keep_ref[...], back_ref[...]
    state = jnp.concatenate([jnp.where(zero, keep, back), jnp.where(zero, back, keep)], axis=1)
    for s in range(reach):
        state += jnp.exp(rate * (s + 1.0)) * product[s : s + 1, :]
    owner = spot(1, chan) // per
    spread = jnp.concatenate([jnp.where(owner == g, state, 0.0) for g in range(groups)], axis=0)
    high, low = split(spread)
    rise = high_ref[...]
    sums[...] = base_ref[...] + (dot(rise, high) + dot(low_ref[...], high) + dot(rise, low))
    start = sums[0:HALO, :] + skip_ref[...] * product
    for ahead in range(1, reach):
        above = jnp.sum(weight * jnp.exp(rate * float(ahead)), axis=0, keepdims=True)
        start -= above * shift[ahead : ahead + HALO, :]
    sums[...] = query_ref[...] * sums[...]
    sums[0:HALO, :] = query * start
    gated[...] = sums[...].astype(BF16)

    sent = copies(staged, out_hbm, 1, steps, sems.at[1])
    for k in range(steps):
        source, first = near_ref, k * block
        if first >= kept:
            source, first = w_ref, first - kept
            weights[first // block].wait()
        made = dot(gated[...], source[:, first : first + block])
        staged[:, k * block : (k + 1) * block] = made.astype(BF16)
        sent[k].start()
    for copy in sent:
        copy.wait()


VMEM = pl.BlockSpec(memory_space=pltpu.VMEM)
SMEM = pl.BlockSpec(memory_space=pltpu.SMEM)
ANY = pl.BlockSpec(memory_space=pl.ANY)


def call(kernel, name, specs, outs, scratch=(), limit=40, flops=0, size=0, out_specs=None):
    return pl.pallas_call(
        kernel,
        in_specs=specs,
        out_specs=out_specs or [VMEM] * len(outs),
        out_shape=outs,
        scratch_shapes=list(scratch),
        compiler_params=pltpu.CompilerParams(vmem_limit_bytes=limit * MIB),
        cost_estimate=pl.CostEstimate(flops=flops, bytes_accessed=size, transcendentals=0),
        name=name,
    )


def in_hbm(value):
    return pltpu.with_memory_space_constraint(value, pltpu.HBM)


def on_device(hidden, norm_gain, w_in, w_short, residues, rates, skip, w_out):
    rows, width = hidden.shape
    columns = w_in.shape[1]
    chan = columns // 3
    half = chan // 2
    groups, modes = rates.shape
    per = chan // groups
    reach = w_short.shape[1] - 1
    devices = lax.axis_size("tm")
    here = lax.axis_index("tm")
    along = 4
    place = jnp.stack([here % 2, here // 2 % along, here // (2 * along)]).astype(jnp.int32)
    gain = norm_gain[None, :]
    taps = w_short.T
    skips = skip[None, :]
    vmem, sem = pltpu.VMEM, pltpu.SemaphoreType.DMA

    product, inv, edges, own, other = call(
        state_kernel,
        "state",
        [SMEM] + [ANY] * 5,
        [
            vmem((rows, chan), BF16),
            vmem((rows, 128), F32),
            vmem((2 * HALO, 2 * chan), F32),
            vmem((modes + 4 * HALO, half), F32),
            vmem((modes + 4 * HALO, half), F32),
        ],
        [
            vmem((rows, width), BF16),
            vmem((width, 2 * chan), BF16),
            vmem((1, width), F32),
            vmem((reach + 1, columns), F32),
            vmem((groups, modes), F32),
            vmem((rows, 2 * chan), F32),
            vmem((HALO + rows, 2 * chan), F32),
            vmem((2 * HALO, 2 * chan), F32),
            sem((3, 8)),
        ],
        flops=4 * rows * width * chan,
        size=2 * width * (rows + 2 * chan),
    )(place, in_hbm(hidden), in_hbm(gain), in_hbm(w_in), in_hbm(taps), in_hbm(rates))

    pairs = [(i, i ^ 1) for i in range(devices)]
    got = lax.ppermute(other, "tm", pairs)
    first, chip = call(
        functools.partial(chip_kernel, hop=float(rows), per=per),
        "chip",
        [SMEM] + [VMEM] * 3,
        [vmem((modes, half), F32), vmem((modes + 4 * HALO, half), F32)],
    )(place, own, got, rates)
    lines = [
        lax.ppermute(chip, "tm", [(i, i ^ (2 * m)) for i in range(devices)])
        for m in range(1, along)
    ]

    query, head, tail = call(
        query_kernel,
        "query",
        [VMEM, ANY, VMEM, ANY] + [VMEM] * 3,
        [vmem((rows, chan), F32), vmem((HALO, columns), F32), vmem((HALO, columns), BF16)],
        [
            vmem((rows, width), BF16),
            vmem((width, chan), BF16),
            vmem((rows, chan), F32),
            vmem((HALO + rows, chan), F32),
            sem((2, 8)),
        ],
        flops=2 * rows * width * chan,
        size=2 * width * (rows + chan),
    )(first, in_hbm(hidden), gain, in_hbm(w_in), taps, inv, edges)
    spread, inner, early, tail = call(
        functools.partial(line_kernel, hop=float(rows), reach=reach, per=per, along=along),
        "line",
        [SMEM] + [VMEM] * (along + 2),
        [
            jax.ShapeDtypeStruct((devices // 2 // along, modes + 4 * reach, half), BF16),
            vmem((modes + 4 * HALO, half), F32),
            vmem((2 * HALO, half), F32),
            vmem((HALO, columns), BF16),
        ],
    )(place, chip, *lines, rates, tail)
    members = [list(range(c, devices, 2 * along)) for c in range(2 * along)]
    gathered = lax.all_to_all(spread, "tm", 0, 0, tiled=True, axis_index_groups=members)
    halo = lax.ppermute(tail, "tm", [(i, i + 1) for i in range(devices - 1)])

    weights = residues * jnp.sqrt(2.0 * rates)
    kept = w_out.shape[1] * 3 // 8
    base, high, low, w_near = call(
        local_kernel,
        "local",
        [VMEM] * 7 + [ANY],
        [
            vmem((rows, chan), F32),
            vmem((rows, groups * modes), BF16),
            vmem((rows, groups * modes), BF16),
            vmem((chan, kept), BF16),
        ],
        [sem],
        flops=2 * rows * rows * chan,
        size=6 * rows * chan,
    )(
        tail, product, skips, rates, residues, rates.reshape(1, -1), weights.reshape(1, -1),
        in_hbm(w_out),
    )

    keep, send = call(
        functools.partial(prefix_kernel, hop=float(rows), reach=reach, per=per, along=along),
        "prefix",
        [SMEM] + [VMEM] * 6,
        [vmem((modes, half), F32)] * 2,
        [
            vmem((devices // 2 // along, HALO, half), F32),
            vmem((devices // 2 // along, 2 * HALO, half), F32),
        ],
    )(place, gathered, rates, first, inner, early, low)
    back = lax.ppermute(send, "tm", pairs)

    return call(
        mix_kernel,
        "mix",
        [SMEM] + [VMEM] * 13 + [ANY],
        jax.ShapeDtypeStruct((rows, w_out.shape[1]), BF16),
        [
            vmem((chan, w_out.shape[1] - kept), BF16),
            vmem((rows, w_out.shape[1]), BF16),
            vmem((rows, chan), BF16),
            vmem((2 * HALO, columns), F32),
            vmem((2 * HALO, chan), F32),
            vmem((rows, chan), F32),
            sem((2, 8)),
        ],
        out_specs=ANY,
    )(
        place, query, base, keep, back, high, low, head, halo, taps, skips, rates, residues,
        w_near, in_hbm(w_out),
    )


def solution(mesh):
    return jax.shard_map(
        on_device,
        mesh=mesh,
        in_specs=(P("tm", None), P(), P(), P(), P(), P(), P(), P()),
        out_specs=P("tm", None),
        check_vma=False,
    )
```

```python
import functools

import jax
import jax.numpy as jnp
from jax import lax
from jax.experimental import pallas as pl
from jax.experimental.pallas import tpu as pltpu
from jax.sharding import PartitionSpec as P

F32 = jnp.float32
BF16 = jnp.bfloat16
HALO = 8
MIB = 1 << 20


def split(value):
    high = value.astype(BF16)
    return high, (value - high.astype(F32)).astype(BF16)


def dot(left, right):
    return jnp.dot(left, right, preferred_element_type=F32)


def spot(axis, count):
    shape = (1, count) if axis else (count, 1)
    return lax.broadcasted_iota(jnp.int32, shape, axis)


def copies(source, target, axis, count, sems):
    size = source.shape[axis] // count
    made = []
    for k in range(count):
        part = pl.ds(k * size, size)
        index = (part, slice(None)) if axis == 0 else (slice(None), part)
        made.append(pltpu.make_async_copy(source.at[index], target.at[index], sems.at[k]))
    return made


def column(table):
    groups, modes = table.shape
    rows = jnp.concatenate(
        [jnp.broadcast_to(table[g : g + 1, :], (modes, modes)) for g in range(groups)], axis=0
    )
    mine = spot(1, modes) == lax.rem(spot(0, groups * modes), modes)
    return jnp.sum(jnp.where(mine, rows, 0.0), axis=1, keepdims=True)


def fold(stacked, modes, per):
    width = stacked.shape[1]
    owner = spot(1, width) // per
    total = jnp.zeros((modes, width), F32)
    for g in range(stacked.shape[0] // modes):
        total = jnp.where(owner == g, stacked[g * modes : (g + 1) * modes, :], total)
    return total


def by_channel(col, modes, per, width):
    return fold(jnp.broadcast_to(col, (col.shape[0], width)), modes, per)


def feature(taps, ext, here, first, width, at=0):
    cols = slice(at, at + width)
    wide = slice(first, first + width)
    total = taps[0:1, wide] * ext[HALO + here.start : HALO + here.stop, cols]
    for k in range(1, taps.shape[0]):
        near = ext[HALO + here.start - k : HALO + here.stop - k, cols]
        total = total + taps[k : k + 1, wide] * near
    return total


EDGE = slice(0, HALO)


def multiply(hidden, inv, gain, near, total, weights, store, lines=(), late=1):
    rows = hidden.shape[0]
    count = len(weights)
    block = near.shape[0] // count
    part = rows // 3
    parts = [slice(first, first + part) for first in range(0, rows, part)]

    def made(here, k):
        cols = slice(k * block, (k + 1) * block)
        scale = jnp.concatenate([inv[here, :]] * (block // 128), axis=1)
        normed = (hidden[here, cols].astype(F32) * scale * gain[:, cols]).astype(BF16)
        return dot(normed, near[cols, :])

    def arrive(k):
        for copy in lines[k : k + 1]:
            copy.wait()
        weights[k].wait()

    for k in range(count - late):
        arrive(k)
        for here in parts:
            if k == 0:
                total[here, :] = made(here, k)
            else:
                total[here, :] += made(here, k)
    for here in parts:
        value = total[here, :]
        for k in range(count - late, count):
            if here.start == 0:
                arrive(k)
            value += made(here, k)
        store(here, value.astype(BF16))


def state_kernel(
    hidden_hbm, gain_hbm, w_hbm, taps_hbm, rates_hbm,
    prod_ref, inv_ref, edge_ref, own_ref,
    hidden, near, gain, taps, rates, total, ext, little, sems,
):
    rows, width = hidden.shape
    chan = prod_ref.shape[1]
    reach = taps.shape[0] - 1
    small = [
        pltpu.make_async_copy(source, target, sems.at[2, k])
        for k, (source, target) in enumerate(
            ((gain_hbm, gain), (taps_hbm, taps), (rates_hbm, rates))
        )
    ]
    lines = copies(hidden_hbm, hidden, 1, 8, sems.at[0])
    weights = copies(w_hbm.at[:, pl.ds(chan, 2 * chan)], near, 0, 8, sems.at[1])
    for copy in small + lines:
        copy.start()
    inv_ref[...] = jnp.zeros_like(inv_ref)
    ext[0:HALO, :] = jnp.zeros((HALO, 2 * chan), F32)
    for copy in small:
        copy.wait()
    modes = rates.shape[1]
    left = (rows - 1 - spot(1, rows)).astype(F32)
    high, low = split(jnp.exp(-column(rates[...]) * left))
    block = width // len(lines)
    for k, copy in enumerate(lines):
        copy.wait()
        weights[k].start()

        def add(i, _, k=k):
            cols = pl.ds(pl.multiple_of(k * block + i * 256, 256), 256)
            wide = hidden[:, cols].astype(F32)
            square = wide * wide
            inv_ref[...] += square[:, :128] + square[:, 128:]
            return 0

        lax.fori_loop(0, block // 256, add, 0)
    inv = lax.rsqrt(jnp.sum(inv_ref[...], axis=1, keepdims=True) / width + 1e-06)
    inv_ref[...] = jnp.broadcast_to(inv, inv_ref.shape)
    crossed, heads = [], []

    def store(here, value):
        ext[HALO + here.start : HALO + here.stop, :] = value.astype(F32)
        key = feature(taps, ext, here, chan, chan, 0)
        value = feature(taps, ext, here, 2 * chan, chan, chan)
        product = key * value
        if here.start == 0:
            early = spot(0, HALO) < reach
            heads.extend(jnp.where(early, kind[0:HALO, :], 0.0) for kind in (key, value))
            product = jnp.where(spot(0, here.stop) >= reach, product, 0.0)
        product = product.astype(BF16)
        prod_ref[here, :] = product
        crossed.append(dot(high[:, here], product) + dot(low[:, here], product))

    multiply(hidden, inv_ref, gain, near, total, weights, store, late=4)

    edge_ref[0:HALO, :] = ext[HALO : 2 * HALO, :]
    edge_ref[HALO:, :] = ext[rows : rows + HALO, :]
    little[0:HALO, :] = ext[rows : rows + HALO, :]
    little[HALO:, :] = jnp.zeros((HALO, 2 * chan), F32)
    tail_k = feature(taps, little, EDGE, chan, chan, 0)
    tail_v = feature(taps, little, EDGE, 2 * chan, chan, chan)
    state = fold(sum(crossed[1:], crossed[0]), modes, chan // rates.shape[0])
    own_ref[...] = jnp.concatenate([state] + heads + [tail_k, tail_v], axis=0)


def joined(tail_k, head_k, tail_v, head_v):
    return ((tail_k + head_k) * (tail_v + head_v)).astype(BF16).astype(F32)


def part(value, modes, k):
    return value[modes + k * HALO : modes + (k + 1) * HALO]


def merge(left, right, rate, length):
    modes = rate.shape[0]
    seam = joined(*[part(v, modes, k) for v, k in ((left, 2), (right, 0), (left, 3), (right, 1))])
    state = jnp.exp(-rate * length) * left[:modes] + right[:modes] + entering(seam, rate, length)
    return jnp.concatenate(
        [state, left[modes : modes + 2 * HALO], right[modes + 2 * HALO :]], axis=0
    )


def entering(seam, rate, length):
    total = jnp.zeros(rate.shape, F32)
    for s in range(HALO - 2):
        total += jnp.exp(-rate * (length - 1.0 - s)) * seam[s : s + 1]
    return total


def chip_kernel(place_ref, own_ref, got_ref, rates_ref, first_ref, chip_ref, *, hop, per):
    zero = place_ref[0:1, :] == 0
    own, got = own_ref[...], got_ref[...]
    first = jnp.where(zero, own, got)
    second = jnp.where(zero, got, own)
    modes, width = first_ref.shape
    rate = by_channel(column(rates_ref[...]), modes, per, width)
    first_ref[...] = first[:modes]
    chip_ref[...] = merge(first, second, rate, hop)


def line_kernel(place_ref, own_ref, *refs, hop, reach, per, along):
    got_refs, (rates_ref, tail_ref, spread_ref, inner_ref, early_ref, sent_ref) = (
        refs[: along - 1], refs[along - 1 :]
    )
    sent_ref[...] = tail_ref[...]
    own = own_ref[...]
    modes = rates_ref.shape[1]
    rate = by_channel(column(rates_ref[...]), modes, per, own.shape[1])
    spot_x = place_ref[1:2, :]
    chips = []
    for j in range(along):
        chip = own
        for m in range(1, along):
            chip = jnp.where(spot_x == (j ^ m), got_refs[m - 1][...], chip)
        chips.append(chip)
    total = chips[0]
    before = jnp.zeros_like(total)
    for j in range(1, along):
        before = jnp.where(spot_x == j, total, before)
        total = merge(total, chips[j], rate, 2.0 * hop)
    inner_ref[...] = before
    early_ref[...] = own[modes : modes + 2 * HALO]
    pieces = [total[:modes]] + [part(total, modes, k)[:reach] for k in range(4)]
    packed = jnp.concatenate(pieces, axis=0).astype(BF16)
    spread_ref[...] = jnp.broadcast_to(packed[None], spread_ref.shape)


def query_kernel(
    after_ref, hidden_hbm, gain_ref, w_hbm, taps_ref, inv_ref, edge_ref,
    query_ref, head_ref, tail_ref, hidden, near, total, ext, sems,
):
    rows, _ = hidden.shape
    chan = query_ref.shape[1]
    lines = copies(hidden_hbm, hidden, 1, 8, sems.at[0])
    weights = copies(w_hbm.at[:, pl.ds(0, chan)], near, 0, 8, sems.at[1])
    for line, weight in zip(lines, weights):
        line.start()
        weight.start()

    def store(here, value):
        ext[HALO + here.start : HALO + here.stop, :] = value.astype(F32)
        query_ref[here, :] = feature(taps_ref, ext, here, 0, chan, 0)

    ext[0:HALO, :] = jnp.zeros((HALO, chan), F32)
    multiply(hidden, inv_ref, gain_ref, near, total, weights, store, lines)
    head_ref[:, :chan] = ext[HALO : 2 * HALO, :]
    head_ref[:, chan:] = edge_ref[0:HALO, :]
    tail = jnp.concatenate([ext[rows : rows + HALO, :], edge_ref[HALO:, :]], axis=1)
    tail_ref[...] = tail.astype(BF16)


def local_kernel(
    after_ref, prod_ref, skip_ref, rates_ref, residues_ref, rrow_ref, wrow_ref, w_hbm,
    base_ref, high_ref, low_ref, near_ref, sem,
):
    fetch = pltpu.make_async_copy(w_hbm.at[:, pl.ds(0, near_ref.shape[1])], near_ref, sem)
    fetch.start()
    rows, chan = prod_ref.shape
    groups, modes = rates_ref.shape
    times = spot(0, rows).astype(F32) + 1.0
    high, low = split(wrow_ref[...] * jnp.exp(-rrow_ref[...] * times))
    high_ref[...] = high
    low_ref[...] = low
    rcol = column(rates_ref[...])
    wcol = column(residues_ref[...]) * jnp.sqrt(2.0 * rcol)
    block = 128
    per = chan // groups
    places = [slice(first, first + block) for first in range(0, rows, block)]
    for here in places:
        base_ref[here, :] = skip_ref[...] * prod_ref[here, :].astype(F32)

    keep = spot(1, chan) // per == spot(0, groups * modes) // modes
    leave_high, leave_low = split(jnp.exp(-rcol * (block - 1 - spot(1, block)).astype(F32)))
    fall = jnp.exp(-rcol * float(block))
    state = jnp.zeros((groups * modes, chan), F32)
    for here, following in zip(places, places[1:]):
        mine = prod_ref[here, :]
        state = fall * state + (dot(leave_high, mine) + dot(leave_low, mine))
        near_high, near_low = split(jnp.where(keep, state, 0.0))
        rise = high[:block, :]
        base_ref[following, :] += (
            dot(rise, near_high) + dot(low[:block, :], near_high) + dot(rise, near_low)
        )

    span = 2 * block
    spots = spot(1, span)
    lags = jnp.where(spots == 0, 0, span - spots)
    terms = wcol * jnp.exp(-rcol * lags.astype(F32))
    terms = jnp.where((spots == 0) | (spots > block), terms, 0.0)
    for g in range(groups):
        filt = jnp.sum(terms[g * modes : (g + 1) * modes, :], axis=0, keepdims=True)
        wide = jnp.broadcast_to(filt, (block, span))
        square = pltpu.roll(wide, 0, 1, stride=1, stride_axis=0)[:, :block].astype(BF16)
        cols = slice(g * per, (g + 1) * per)
        for here in places:
            base_ref[here, cols] += dot(square, prod_ref[here, cols])
    fetch.wait()


def prefix_kernel(
    place_ref, all_ref, rates_ref, first_ref, inner_ref, early_ref, after_ref,
    state_ref, seams, tails, *, hop, reach, per, along,
):
    count = all_ref.shape[0]
    modes, width = state_ref.shape
    zero, spot_x, line = place_ref[0:1, :] == 0, place_ref[1:2, :], place_ref[2:3, :]
    col = column(rates_ref[...])
    rate = by_channel(col, modes, per, width)
    span = 2.0 * hop * along
    fall = jnp.exp(-rate * span)
    wide = all_ref[...].astype(F32)

    def piece(k):
        return wide[:, modes + k * reach : modes + (k + 1) * reach, :]

    def before(k):
        value = piece(k)
        return jnp.concatenate([jnp.zeros_like(value[:1]), value[:-1]], axis=0)

    seams[...] = jnp.zeros_like(seams)
    tails[...] = jnp.zeros_like(tails)
    tail_k, tail_v = before(2), before(3)
    tails[:, 0:reach, :] = tail_k
    tails[:, HALO : HALO + reach, :] = tail_v
    seams[:, 0:reach, :] = joined(tail_k, piece(0), tail_v, piece(1))
    total = jnp.zeros((modes, width), F32)
    for j in range(count):
        total = jnp.where(j < line, fall * total + wide[j, :modes, :], total)
    index = spot(1, count * HALO)
    place, step = index // HALO, lax.rem(index, HALO)
    level = line[:, : count * HALO]
    lag = span * (level - 1 - place).astype(F32) + (span - 1.0) - step.astype(F32)
    fade = jnp.where(place < level, jnp.exp(-col * jnp.maximum(lag, 0.0)), 0.0)
    high, low = split(fade)
    products = seams[...].reshape(count * HALO, width).astype(BF16)
    total += fold(dot(high, products) + dot(low, products), modes, per)

    inner, early = inner_ref[...], early_ref[...]
    outer = tails[0]
    for j in range(1, count):
        outer = jnp.where(line == j, tails[j], outer)
    heads = [part(inner, modes, k) for k in (0, 1)]
    seam = joined(outer[:HALO], heads[0], outer[HALO:], heads[1])
    length = 2.0 * hop * spot_x.astype(F32)
    within = jnp.exp(-rate * length) * total + inner[:modes]
    for s in range(reach):
        within += jnp.exp(-rate * jnp.maximum(length - 1.0 - s, 0.0)) * seam[s : s + 1]
    starts = spot_x == 0
    total = jnp.where(starts, total, within)
    last_k = jnp.where(starts, outer[:HALO], part(inner, modes, 2))
    last_v = jnp.where(starts, outer[HALO:], part(inner, modes, 3))
    seam = joined(last_k, early[:HALO], last_v, early[HALO:])
    following = jnp.exp(-rate * hop) * total + first_ref[...] + entering(seam, rate, hop)
    state_ref[...] = jnp.where(zero, total, following)


def mix_kernel(
    query_ref, base_ref, state_ref, high_ref, low_ref, head_ref, halo_ref,
    taps_ref, skip_ref, rates_ref, residues_ref, near_ref, w_hbm,
    out_hbm, w_ref, staged, gated, ext, shift, sums, sems,
):
    steps = sems.shape[1]
    kept = near_ref.shape[1]
    block = out_hbm.shape[1] // steps
    rest = w_ref.shape[1]
    weights = copies(w_hbm.at[:, pl.ds(kept, rest)], w_ref, 1, rest // block, sems.at[0])
    for copy in weights:
        copy.start()
    rows, chan = query_ref.shape
    groups, modes = rates_ref.shape
    per = chan // groups
    reach = taps_ref.shape[0] - 1
    ext[0:HALO, :] = halo_ref[...].astype(F32)
    ext[HALO:, :] = head_ref[...]
    query, key, value = [feature(taps_ref, ext, EDGE, n * chan, chan, n * chan) for n in range(3)]
    product = jnp.where(spot(0, HALO) < reach, key * value, 0.0).astype(BF16).astype(F32)
    shift[0:HALO, :] = product
    shift[HALO:, :] = jnp.zeros((HALO, chan), F32)
    rcol = column(rates_ref[...])
    wcol = column(residues_ref[...]) * jnp.sqrt(2.0 * rcol)
    rate = by_channel(rcol, modes, per, chan)
    weight = by_channel(wcol, modes, per, chan)

    state = state_ref[...]
    for s in range(reach):
        state += jnp.exp(rate * (s + 1.0)) * product[s : s + 1, :]
    owner = spot(1, chan) // per
    spread = jnp.concatenate([jnp.where(owner == g, state, 0.0) for g in range(groups)], axis=0)
    high, low = split(spread)
    rise = high_ref[...]
    sums[...] = base_ref[...] + (dot(rise, high) + dot(low_ref[...], high) + dot(rise, low))
    start = sums[0:HALO, :] + skip_ref[...] * product
    for ahead in range(1, reach):
        above = jnp.sum(weight * jnp.exp(rate * float(ahead)), axis=0, keepdims=True)
        start -= above * shift[ahead : ahead + HALO, :]
    sums[...] = query_ref[...] * sums[...]
    sums[0:HALO, :] = query * start
    gated[...] = sums[...].astype(BF16)

    sent = copies(staged, out_hbm, 1, steps, sems.at[1])
    for k in range(steps):
        source, first = near_ref, k * block
        if first >= kept:
            source, first = w_ref, first - kept
            weights[first // block].wait()
        made = dot(gated[...], source[:, first : first + block])
        staged[:, k * block : (k + 1) * block] = made.astype(BF16)
        sent[k].start()
    for copy in sent:
        copy.wait()


VMEM = pl.BlockSpec(memory_space=pltpu.VMEM)
ANY = pl.BlockSpec(memory_space=pl.ANY)


def call(kernel, name, specs, outs, scratch=(), limit=40, flops=0, size=0, out_specs=None):
    return pl.pallas_call(
        kernel,
        in_specs=specs,
        out_specs=out_specs or [VMEM] * len(outs),
        out_shape=outs,
        scratch_shapes=list(scratch),
        compiler_params=pltpu.CompilerParams(vmem_limit_bytes=limit * MIB),
        cost_estimate=pl.CostEstimate(flops=flops, bytes_accessed=size, transcendentals=0),
        name=name,
    )


def in_hbm(value):
    return pltpu.with_memory_space_constraint(value, pltpu.HBM)


def on_device(hidden, norm_gain, w_in, w_short, residues, rates, skip, w_out):
    rows, width = hidden.shape
    columns = w_in.shape[1]
    chan = columns // 3
    groups, modes = rates.shape
    per = chan // groups
    reach = w_short.shape[1] - 1
    devices = lax.axis_size("tm")
    here = lax.axis_index("tm")
    along = 4
    place = jnp.stack([here % 2, here // 2 % along, here // (2 * along)]).astype(jnp.int32)
    place = jnp.broadcast_to(place[:, None], (3, chan))
    gain = norm_gain[None, :]
    taps = w_short.T
    skips = skip[None, :]
    vmem, sem = pltpu.VMEM, pltpu.SemaphoreType.DMA

    product, inv, edges, own = call(
        state_kernel,
        "state",
        [ANY] * 5,
        [
            vmem((rows, chan), BF16),
            vmem((rows, 128), F32),
            vmem((2 * HALO, 2 * chan), F32),
            vmem((modes + 4 * HALO, chan), F32),
        ],
        [
            vmem((rows, width), BF16),
            vmem((width, 2 * chan), BF16),
            vmem((1, width), F32),
            vmem((reach + 1, columns), F32),
            vmem((groups, modes), F32),
            vmem((rows, 2 * chan), F32),
            vmem((HALO + rows, 2 * chan), F32),
            vmem((2 * HALO, 2 * chan), F32),
            sem((3, 8)),
        ],
        flops=4 * rows * width * chan,
        size=2 * width * (rows + 2 * chan),
    )(in_hbm(hidden), in_hbm(gain), in_hbm(w_in), in_hbm(taps), in_hbm(rates))

    pairs = [(i, i ^ 1) for i in range(devices)]
    got = lax.ppermute(own, "tm", pairs)
    first, chip = call(
        functools.partial(chip_kernel, hop=float(rows), per=per),
        "chip",
        [VMEM] + [VMEM] * 3,
        [vmem((modes, chan), F32), vmem((modes + 4 * HALO, chan), F32)],
    )(place, own, got, rates)
    lines = [
        lax.ppermute(chip, "tm", [(i, i ^ (2 * m)) for i in range(devices)])
        for m in range(1, along)
    ]

    query, head, tail = call(
        query_kernel,
        "query",
        [VMEM, ANY, VMEM, ANY] + [VMEM] * 3,
        [vmem((rows, chan), F32), vmem((HALO, columns), F32), vmem((HALO, columns), BF16)],
        [
            vmem((rows, width), BF16),
            vmem((width, chan), BF16),
            vmem((rows, chan), F32),
            vmem((HALO + rows, chan), F32),
            sem((2, 8)),
        ],
        flops=2 * rows * width * chan,
        size=2 * width * (rows + chan),
    )(first, in_hbm(hidden), gain, in_hbm(w_in), taps, inv, edges)
    spread, inner, early, tail = call(
        functools.partial(line_kernel, hop=float(rows), reach=reach, per=per, along=along),
        "line",
        [VMEM] + [VMEM] * (along + 2),
        [
            jax.ShapeDtypeStruct((devices // 2 // along, modes + 4 * reach, chan), BF16),
            vmem((modes + 4 * HALO, chan), F32),
            vmem((2 * HALO, chan), F32),
            vmem((HALO, columns), BF16),
        ],
    )(place, chip, *lines, rates, tail)
    members = [list(range(c, devices, 2 * along)) for c in range(2 * along)]
    gathered = lax.all_to_all(spread, "tm", 0, 0, tiled=True, axis_index_groups=members)
    halo = lax.ppermute(tail, "tm", [(i, i + 1) for i in range(devices - 1)])

    weights = residues * jnp.sqrt(2.0 * rates)
    kept = w_out.shape[1] * 3 // 8
    base, high, low, w_near = call(
        local_kernel,
        "local",
        [VMEM] * 7 + [ANY],
        [
            vmem((rows, chan), F32),
            vmem((rows, groups * modes), BF16),
            vmem((rows, groups * modes), BF16),
            vmem((chan, kept), BF16),
        ],
        [sem],
        flops=2 * rows * rows * chan,
        size=6 * rows * chan,
    )(
        tail, product, skips, rates, residues, rates.reshape(1, -1), weights.reshape(1, -1),
        in_hbm(w_out),
    )

    state, = call(
        functools.partial(prefix_kernel, hop=float(rows), reach=reach, per=per, along=along),
        "prefix",
        [VMEM] + [VMEM] * 6,
        [vmem((modes, chan), F32)],
        [
            vmem((devices // 2 // along, HALO, chan), F32),
            vmem((devices // 2 // along, 2 * HALO, chan), F32),
        ],
    )(place, gathered, rates, first, inner, early, low)

    return call(
        mix_kernel,
        "mix",
        [VMEM] * 12 + [ANY],
        jax.ShapeDtypeStruct((rows, w_out.shape[1]), BF16),
        [
            vmem((chan, w_out.shape[1] - kept), BF16),
            vmem((rows, w_out.shape[1]), BF16),
            vmem((rows, chan), BF16),
            vmem((2 * HALO, columns), F32),
            vmem((2 * HALO, chan), F32),
            vmem((rows, chan), F32),
            sem((2, 8)),
        ],
        out_specs=ANY,
    )(
        query, base, state, high, low, head, halo, taps, skips, rates, residues,
        w_near, in_hbm(w_out),
    )


def solution(mesh):
    return jax.shard_map(
        on_device,
        mesh=mesh,
        in_specs=(P("tm", None), P(), P(), P(), P(), P(), P(), P()),
        out_specs=P("tm", None),
        check_vma=False,
    )
```

```python
import functools

import jax
import jax.numpy as jnp
from jax import lax
from jax.experimental import pallas as pl
from jax.experimental.pallas import tpu as pltpu
from jax.sharding import PartitionSpec as P

F32 = jnp.float32
BF16 = jnp.bfloat16
HALO = 8
MIB = 1 << 20


def split(value):
    high = value.astype(BF16)
    return high, (value - high.astype(F32)).astype(BF16)


def dot(left, right):
    return jnp.dot(left, right, preferred_element_type=F32)


def spot(axis, count):
    shape = (1, count) if axis else (count, 1)
    return lax.broadcasted_iota(jnp.int32, shape, axis)


def copies(source, target, axis, count, sems):
    size = source.shape[axis] // count
    made = []
    for k in range(count):
        part = pl.ds(k * size, size)
        index = (part, slice(None)) if axis == 0 else (slice(None), part)
        made.append(pltpu.make_async_copy(source.at[index], target.at[index], sems.at[k]))
    return made


def column(table):
    groups, modes = table.shape
    rows = jnp.concatenate(
        [jnp.broadcast_to(table[g : g + 1, :], (modes, modes)) for g in range(groups)], axis=0
    )
    mine = spot(1, modes) == lax.rem(spot(0, groups * modes), modes)
    return jnp.sum(jnp.where(mine, rows, 0.0), axis=1, keepdims=True)


def fold(stacked, modes, per):
    width = stacked.shape[1]
    owner = spot(1, width) // per
    total = jnp.zeros((modes, width), F32)
    for g in range(stacked.shape[0] // modes):
        total = jnp.where(owner == g, stacked[g * modes : (g + 1) * modes, :], total)
    return total


def by_channel(col, modes, per, width):
    return fold(jnp.broadcast_to(col, (col.shape[0], width)), modes, per)


def feature(taps, ext, here, first, width, at=0):
    cols = slice(at, at + width)
    wide = slice(first, first + width)
    total = taps[0:1, wide] * ext[HALO + here.start : HALO + here.stop, cols]
    for k in range(1, taps.shape[0]):
        near = ext[HALO + here.start - k : HALO + here.stop - k, cols]
        total = total + taps[k : k + 1, wide] * near
    return total


EDGE = slice(0, HALO)


def multiply(hidden, inv, gain, near, total, arrive, store, late=1, count=8):
    rows, width = hidden.shape
    block = width // count
    part = rows // 3
    parts = [slice(first, first + part) for first in range(0, rows, part)]

    def made(here, k):
        cols = slice(k * block, (k + 1) * block)
        scale = jnp.concatenate([inv[here, :]] * (block // 128), axis=1)
        normed = (hidden[here, cols].astype(F32) * scale * gain[:, cols]).astype(BF16)
        return dot(normed, near(cols))

    for k in range(count - late):
        arrive(k)
        for here in parts:
            if k == 0:
                total[here, :] = made(here, k)
            else:
                total[here, :] += made(here, k)
    for here in parts:
        value = total[here, :]
        for k in range(count - late, count):
            if here.start == 0:
                arrive(k)
            value += made(here, k)
        store(here, value.astype(BF16))


def state_kernel(
    hidden_hbm, gain_hbm, w_hbm, taps_hbm, rates_hbm,
    prod_ref, inv_ref, edge_ref, own_ref, ahead_ref,
    hidden, near, gain, taps, rates, total, ext, little, sems,
):
    rows, width = hidden.shape
    chan = prod_ref.shape[1]
    reach = taps.shape[0] - 1
    small = [
        pltpu.make_async_copy(source, target, sems.at[2, k])
        for k, (source, target) in enumerate(
            ((gain_hbm, gain), (taps_hbm, taps), (rates_hbm, rates))
        )
    ]
    lines = copies(hidden_hbm, hidden, 1, 8, sems.at[0])
    weights = copies(w_hbm.at[:, pl.ds(chan, 2 * chan)], near, 0, 8, sems.at[1])
    for copy in small + lines:
        copy.start()
    inv_ref[...] = jnp.zeros_like(inv_ref)
    ext[0:HALO, :] = jnp.zeros((HALO, 2 * chan), F32)
    for copy in small:
        copy.wait()
    modes = rates.shape[1]
    left = (rows - 1 - spot(1, rows)).astype(F32)
    high, low = split(jnp.exp(-column(rates[...]) * left))
    block = width // len(lines)
    for k, copy in enumerate(lines):
        copy.wait()
        weights[k].start()

        def add(i, _, k=k):
            cols = pl.ds(pl.multiple_of(k * block + i * 256, 256), 256)
            wide = hidden[:, cols].astype(F32)
            square = wide * wide
            inv_ref[...] += square[:, :128] + square[:, 128:]
            return 0

        lax.fori_loop(0, block // 256, add, 0)
    inv = lax.rsqrt(jnp.sum(inv_ref[...], axis=1, keepdims=True) / width + 1e-06)
    inv_ref[...] = jnp.broadcast_to(inv, inv_ref.shape)
    crossed, heads = [], []

    def store(here, value):
        ext[HALO + here.start : HALO + here.stop, :] = value.astype(F32)
        key = feature(taps, ext, here, chan, chan, 0)
        value = feature(taps, ext, here, 2 * chan, chan, chan)
        product = key * value
        if here.start == 0:
            early = spot(0, HALO) < reach
            heads.extend(jnp.where(early, kind[0:HALO, :], 0.0) for kind in (key, value))
            product = jnp.where(spot(0, here.stop) >= reach, product, 0.0)
        product = product.astype(BF16)
        prod_ref[here, :] = product
        crossed.append(dot(high[:, here], product) + dot(low[:, here], product))

    deep = ahead_ref.shape[0]
    ahead = pltpu.make_async_copy(
        w_hbm.at[pl.ds(0, deep), pl.ds(0, chan)], ahead_ref, sems.at[2, 7]
    )

    def arrive(k):
        weights[k].wait()
        if k == 6:
            ahead.start()

    def weight_rows(cols):
        return near[cols, :]

    multiply(hidden, inv_ref, gain, weight_rows, total, arrive, store, late=4)

    edge_ref[0:HALO, :] = ext[HALO : 2 * HALO, :]
    edge_ref[HALO:, :] = ext[rows : rows + HALO, :]
    little[0:HALO, :] = ext[rows : rows + HALO, :]
    little[HALO:, :] = jnp.zeros((HALO, 2 * chan), F32)
    tail_k = feature(taps, little, EDGE, chan, chan, 0)
    tail_v = feature(taps, little, EDGE, 2 * chan, chan, chan)
    state = fold(sum(crossed[1:], crossed[0]), modes, chan // rates.shape[0])
    own_ref[...] = jnp.concatenate([state] + heads + [tail_k, tail_v], axis=0)
    ahead.wait()


def joined(tail_k, head_k, tail_v, head_v):
    return ((tail_k + head_k) * (tail_v + head_v)).astype(BF16).astype(F32)


def part(value, modes, k):
    return value[modes + k * HALO : modes + (k + 1) * HALO]


def merge(left, right, rate, length):
    modes = rate.shape[0]
    seam = joined(*[part(v, modes, k) for v, k in ((left, 2), (right, 0), (left, 3), (right, 1))])
    state = jnp.exp(-rate * length) * left[:modes] + right[:modes] + entering(seam, rate, length)
    return jnp.concatenate(
        [state, left[modes : modes + 2 * HALO], right[modes + 2 * HALO :]], axis=0
    )


def entering(seam, rate, length):
    total = jnp.zeros(rate.shape, F32)
    for s in range(HALO - 2):
        total += jnp.exp(-rate * (length - 1.0 - s)) * seam[s : s + 1]
    return total


def chip_kernel(place_ref, own_ref, got_ref, rates_ref, first_ref, chip_ref, *, hop, per):
    zero = place_ref[0:1, :] == 0
    own, got = own_ref[...], got_ref[...]
    first = jnp.where(zero, own, got)
    second = jnp.where(zero, got, own)
    modes, width = first_ref.shape
    rate = by_channel(column(rates_ref[...]), modes, per, width)
    first_ref[...] = first[:modes]
    chip_ref[...] = merge(first, second, rate, hop)


def line_kernel(place_ref, own_ref, *refs, hop, reach, per, along):
    got_refs, (rates_ref, tail_ref, spread_ref, inner_ref, early_ref, sent_ref) = (
        refs[: along - 1], refs[along - 1 :]
    )
    sent_ref[...] = tail_ref[...]
    own = own_ref[...]
    modes = rates_ref.shape[1]
    rate = by_channel(column(rates_ref[...]), modes, per, own.shape[1])
    spot_x = place_ref[1:2, :]
    chips = []
    for j in range(along):
        chip = own
        for m in range(1, along):
            chip = jnp.where(spot_x == (j ^ m), got_refs[m - 1][...], chip)
        chips.append(chip)
    total = chips[0]
    before = jnp.zeros_like(total)
    for j in range(1, along):
        before = jnp.where(spot_x == j, total, before)
        total = merge(total, chips[j], rate, 2.0 * hop)
    inner_ref[...] = before
    early_ref[...] = own[modes : modes + 2 * HALO]
    pieces = [total[:modes]] + [part(total, modes, k)[:reach] for k in range(4)]
    packed = jnp.concatenate(pieces, axis=0).astype(BF16)
    spread_ref[...] = jnp.broadcast_to(packed[None], spread_ref.shape)


def query_kernel(
    after_ref, hidden_hbm, gain_ref, w_hbm, taps_ref, inv_ref, edge_ref, ahead_ref,
    query_ref, head_ref, tail_ref, hidden, near, total, ext, sems,
):
    rows, width = hidden.shape
    chan = query_ref.shape[1]
    deep, rest = ahead_ref.shape[0], near.shape[0]
    count = 8
    known = count * deep // width
    lines = copies(hidden_hbm, hidden, 1, count, sems.at[0])
    source = w_hbm.at[pl.ds(deep, rest), pl.ds(0, chan)]
    weights = copies(source, near, 0, count - known, sems.at[1])
    for k, line in enumerate(lines):
        line.start()
        if k >= known:
            weights[k - known].start()

    def arrive(k):
        lines[k].wait()
        if k >= known:
            weights[k - known].wait()

    def weight_rows(cols):
        if cols.stop <= deep:
            return ahead_ref[cols, :]
        return near[cols.start - deep : cols.stop - deep, :]

    def store(here, value):
        ext[HALO + here.start : HALO + here.stop, :] = value.astype(F32)
        query_ref[here, :] = feature(taps_ref, ext, here, 0, chan, 0)

    ext[0:HALO, :] = jnp.zeros((HALO, chan), F32)
    multiply(hidden, inv_ref, gain_ref, weight_rows, total, arrive, store)
    head_ref[:, :chan] = ext[HALO : 2 * HALO, :]
    head_ref[:, chan:] = edge_ref[0:HALO, :]
    tail = jnp.concatenate([ext[rows : rows + HALO, :], edge_ref[HALO:, :]], axis=1)
    tail_ref[...] = tail.astype(BF16)


def local_kernel(
    after_ref, prod_ref, skip_ref, rates_ref, residues_ref, rrow_ref, wrow_ref, w_hbm,
    base_ref, high_ref, low_ref, near_ref, sem,
):
    fetch = pltpu.make_async_copy(w_hbm.at[:, pl.ds(0, near_ref.shape[1])], near_ref, sem)
    fetch.start()
    rows, chan = prod_ref.shape
    groups, modes = rates_ref.shape
    times = spot(0, rows).astype(F32) + 1.0
    high, low = split(wrow_ref[...] * jnp.exp(-rrow_ref[...] * times))
    high_ref[...] = high
    low_ref[...] = low
    rcol = column(rates_ref[...])
    wcol = column(residues_ref[...]) * jnp.sqrt(2.0 * rcol)
    block = 128
    per = chan // groups
    places = [slice(first, first + block) for first in range(0, rows, block)]
    for here in places:
        base_ref[here, :] = skip_ref[...] * prod_ref[here, :].astype(F32)

    keep = spot(1, chan) // per == spot(0, groups * modes) // modes
    leave_high, leave_low = split(jnp.exp(-rcol * (block - 1 - spot(1, block)).astype(F32)))
    fall = jnp.exp(-rcol * float(block))
    state = jnp.zeros((groups * modes, chan), F32)
    for here, following in zip(places, places[1:]):
        mine = prod_ref[here, :]
        state = fall * state + (dot(leave_high, mine) + dot(leave_low, mine))
        near_high, near_low = split(jnp.where(keep, state, 0.0))
        rise = high[:block, :]
        base_ref[following, :] += (
            dot(rise, near_high) + dot(low[:block, :], near_high) + dot(rise, near_low)
        )

    span = 2 * block
    spots = spot(1, span)
    lags = jnp.where(spots == 0, 0, span - spots)
    terms = wcol * jnp.exp(-rcol * lags.astype(F32))
    terms = jnp.where((spots == 0) | (spots > block), terms, 0.0)
    for g in range(groups):
        filt = jnp.sum(terms[g * modes : (g + 1) * modes, :], axis=0, keepdims=True)
        wide = jnp.broadcast_to(filt, (block, span))
        square = pltpu.roll(wide, 0, 1, stride=1, stride_axis=0)[:, :block].astype(BF16)
        cols = slice(g * per, (g + 1) * per)
        for here in places:
            base_ref[here, cols] += dot(square, prod_ref[here, cols])
    fetch.wait()


def prefix_kernel(
    place_ref, all_ref, rates_ref, first_ref, inner_ref, early_ref, after_ref,
    state_ref, seams, tails, *, hop, reach, per, along,
):
    count = all_ref.shape[0]
    modes, width = state_ref.shape
    zero, spot_x, line = place_ref[0:1, :] == 0, place_ref[1:2, :], place_ref[2:3, :]
    col = column(rates_ref[...])
    rate = by_channel(col, modes, per, width)
    span = 2.0 * hop * along
    fall = jnp.exp(-rate * span)
    wide = all_ref[...].astype(F32)

    def piece(k):
        return wide[:, modes + k * reach : modes + (k + 1) * reach, :]

    def before(k):
        value = piece(k)
        return jnp.concatenate([jnp.zeros_like(value[:1]), value[:-1]], axis=0)

    seams[...] = jnp.zeros_like(seams)
    tails[...] = jnp.zeros_like(tails)
    tail_k, tail_v = before(2), before(3)
    tails[:, 0:reach, :] = tail_k
    tails[:, HALO : HALO + reach, :] = tail_v
    seams[:, 0:reach, :] = joined(tail_k, piece(0), tail_v, piece(1))
    total = jnp.zeros((modes, width), F32)
    for j in range(count):
        total = jnp.where(j < line, fall * total + wide[j, :modes, :], total)
    index = spot(1, count * HALO)
    place, step = index // HALO, lax.rem(index, HALO)
    level = line[:, : count * HALO]
    lag = span * (level - 1 - place).astype(F32) + (span - 1.0) - step.astype(F32)
    fade = jnp.where(place < level, jnp.exp(-col * jnp.maximum(lag, 0.0)), 0.0)
    high, low = split(fade)
    products = seams[...].reshape(count * HALO, width).astype(BF16)
    total += fold(dot(high, products) + dot(low, products), modes, per)

    inner, early = inner_ref[...], early_ref[...]
    outer = tails[0]
    for j in range(1, count):
        outer = jnp.where(line == j, tails[j], outer)
    heads = [part(inner, modes, k) for k in (0, 1)]
    seam = joined(outer[:HALO], heads[0], outer[HALO:], heads[1])
    length = 2.0 * hop * spot_x.astype(F32)
    within = jnp.exp(-rate * length) * total + inner[:modes]
    for s in range(reach):
        within += jnp.exp(-rate * jnp.maximum(length - 1.0 - s, 0.0)) * seam[s : s + 1]
    starts = spot_x == 0
    total = jnp.where(starts, total, within)
    last_k = jnp.where(starts, outer[:HALO], part(inner, modes, 2))
    last_v = jnp.where(starts, outer[HALO:], part(inner, modes, 3))
    seam = joined(last_k, early[:HALO], last_v, early[HALO:])
    following = jnp.exp(-rate * hop) * total + first_ref[...] + entering(seam, rate, hop)
    state_ref[...] = jnp.where(zero, total, following)


def mix_kernel(
    query_ref, base_ref, state_ref, high_ref, low_ref, head_ref, halo_ref,
    taps_ref, skip_ref, rates_ref, residues_ref, near_ref, w_hbm,
    out_hbm, w_ref, staged, gated, ext, shift, sums, sems,
):
    steps = sems.shape[1]
    kept = near_ref.shape[1]
    block = out_hbm.shape[1] // steps
    rest = w_ref.shape[1]
    weights = copies(w_hbm.at[:, pl.ds(kept, rest)], w_ref, 1, rest // block, sems.at[0])
    for copy in weights:
        copy.start()
    rows, chan = query_ref.shape
    groups, modes = rates_ref.shape
    per = chan // groups
    reach = taps_ref.shape[0] - 1
    ext[0:HALO, :] = halo_ref[...].astype(F32)
    ext[HALO:, :] = head_ref[...]
    query, key, value = [feature(taps_ref, ext, EDGE, n * chan, chan, n * chan) for n in range(3)]
    product = jnp.where(spot(0, HALO) < reach, key * value, 0.0).astype(BF16).astype(F32)
    shift[0:HALO, :] = product
    shift[HALO:, :] = jnp.zeros((HALO, chan), F32)
    rcol = column(rates_ref[...])
    wcol = column(residues_ref[...]) * jnp.sqrt(2.0 * rcol)
    rate = by_channel(rcol, modes, per, chan)
    weight = by_channel(wcol, modes, per, chan)

    state = state_ref[...]
    for s in range(reach):
        state += jnp.exp(rate * (s + 1.0)) * product[s : s + 1, :]
    owner = spot(1, chan) // per
    spread = jnp.concatenate([jnp.where(owner == g, state, 0.0) for g in range(groups)], axis=0)
    high, low = split(spread)
    rise = high_ref[...]
    sums[...] = base_ref[...] + (dot(rise, high) + dot(low_ref[...], high) + dot(rise, low))
    start = sums[0:HALO, :] + skip_ref[...] * product
    for ahead in range(1, reach):
        above = jnp.sum(weight * jnp.exp(rate * float(ahead)), axis=0, keepdims=True)
        start -= above * shift[ahead : ahead + HALO, :]
    sums[...] = query_ref[...] * sums[...]
    sums[0:HALO, :] = query * start
    gated[...] = sums[...].astype(BF16)

    sent = copies(staged, out_hbm, 1, steps, sems.at[1])
    for k in range(steps):
        source, first = near_ref, k * block
        if first >= kept:
            source, first = w_ref, first - kept
            weights[first // block].wait()
        made = dot(gated[...], source[:, first : first + block])
        staged[:, k * block : (k + 1) * block] = made.astype(BF16)
        sent[k].start()
    for copy in sent:
        copy.wait()


VMEM = pl.BlockSpec(memory_space=pltpu.VMEM)
ANY = pl.BlockSpec(memory_space=pl.ANY)


def call(kernel, name, specs, outs, scratch=(), limit=40, flops=0, size=0, out_specs=None):
    return pl.pallas_call(
        kernel,
        in_specs=specs,
        out_specs=out_specs or [VMEM] * len(outs),
        out_shape=outs,
        scratch_shapes=list(scratch),
        compiler_params=pltpu.CompilerParams(vmem_limit_bytes=limit * MIB),
        cost_estimate=pl.CostEstimate(flops=flops, bytes_accessed=size, transcendentals=0),
        name=name,
    )


def in_hbm(value):
    return pltpu.with_memory_space_constraint(value, pltpu.HBM)


def on_device(hidden, norm_gain, w_in, w_short, residues, rates, skip, w_out):
    rows, width = hidden.shape
    columns = w_in.shape[1]
    chan = columns // 3
    groups, modes = rates.shape
    per = chan // groups
    reach = w_short.shape[1] - 1
    devices = lax.axis_size("tm")
    here = lax.axis_index("tm")
    along = 4
    place = jnp.stack([here % 2, here // 2 % along, here // (2 * along)]).astype(jnp.int32)
    place = jnp.broadcast_to(place[:, None], (3, chan))
    gain = norm_gain[None, :]
    taps = w_short.T
    skips = skip[None, :]
    vmem, sem = pltpu.VMEM, pltpu.SemaphoreType.DMA

    deep = width // 2
    product, inv, edges, own, ahead = call(
        state_kernel,
        "state",
        [ANY] * 5,
        [
            vmem((rows, chan), BF16),
            vmem((rows, 128), F32),
            vmem((2 * HALO, 2 * chan), F32),
            vmem((modes + 4 * HALO, chan), F32),
            vmem((deep, chan), BF16),
        ],
        [
            vmem((rows, width), BF16),
            vmem((width, 2 * chan), BF16),
            vmem((1, width), F32),
            vmem((reach + 1, columns), F32),
            vmem((groups, modes), F32),
            vmem((rows, 2 * chan), F32),
            vmem((HALO + rows, 2 * chan), F32),
            vmem((2 * HALO, 2 * chan), F32),
            sem((3, 8)),
        ],
        flops=4 * rows * width * chan,
        size=2 * width * (rows + 2 * chan),
    )(in_hbm(hidden), in_hbm(gain), in_hbm(w_in), in_hbm(taps), in_hbm(rates))

    pairs = [(i, i ^ 1) for i in range(devices)]
    got = lax.ppermute(own, "tm", pairs)
    first, chip = call(
        functools.partial(chip_kernel, hop=float(rows), per=per),
        "chip",
        [VMEM] + [VMEM] * 3,
        [vmem((modes, chan), F32), vmem((modes + 4 * HALO, chan), F32)],
    )(place, own, got, rates)
    lines = [
        lax.ppermute(chip, "tm", [(i, i ^ (2 * m)) for i in range(devices)])
        for m in range(1, along)
    ]

    query, head, tail = call(
        query_kernel,
        "query",
        [VMEM, ANY, VMEM, ANY] + [VMEM] * 4,
        [vmem((rows, chan), F32), vmem((HALO, columns), F32), vmem((HALO, columns), BF16)],
        [
            vmem((rows, width), BF16),
            vmem((width - deep, chan), BF16),
            vmem((rows, chan), F32),
            vmem((HALO + rows, chan), F32),
            sem((2, 8)),
        ],
        flops=2 * rows * width * chan,
        size=2 * width * (rows + chan),
    )(first, in_hbm(hidden), gain, in_hbm(w_in), taps, inv, edges, ahead)
    spread, inner, early, tail = call(
        functools.partial(line_kernel, hop=float(rows), reach=reach, per=per, along=along),
        "line",
        [VMEM] + [VMEM] * (along + 2),
        [
            jax.ShapeDtypeStruct((devices // 2 // along, modes + 4 * reach, chan), BF16),
            vmem((modes + 4 * HALO, chan), F32),
            vmem((2 * HALO, chan), F32),
            vmem((HALO, columns), BF16),
        ],
    )(place, chip, *lines, rates, tail)
    members = [list(range(c, devices, 2 * along)) for c in range(2 * along)]
    gathered = lax.all_to_all(spread, "tm", 0, 0, tiled=True, axis_index_groups=members)
    halo = lax.ppermute(tail, "tm", [(i, i + 1) for i in range(devices - 1)])

    weights = residues * jnp.sqrt(2.0 * rates)
    kept = w_out.shape[1] * 3 // 8
    base, high, low, w_near = call(
        local_kernel,
        "local",
        [VMEM] * 7 + [ANY],
        [
            vmem((rows, chan), F32),
            vmem((rows, groups * modes), BF16),
            vmem((rows, groups * modes), BF16),
            vmem((chan, kept), BF16),
        ],
        [sem],
        flops=2 * rows * rows * chan,
        size=6 * rows * chan,
    )(
        tail, product, skips, rates, residues, rates.reshape(1, -1), weights.reshape(1, -1),
        in_hbm(w_out),
    )

    state, = call(
        functools.partial(prefix_kernel, hop=float(rows), reach=reach, per=per, along=along),
        "prefix",
        [VMEM] + [VMEM] * 6,
        [vmem((modes, chan), F32)],
        [
            vmem((devices // 2 // along, HALO, chan), F32),
            vmem((devices // 2 // along, 2 * HALO, chan), F32),
        ],
    )(place, gathered, rates, first, inner, early, low)

    return call(
        mix_kernel,
        "mix",
        [VMEM] * 12 + [ANY],
        jax.ShapeDtypeStruct((rows, w_out.shape[1]), BF16),
        [
            vmem((chan, w_out.shape[1] - kept), BF16),
            vmem((rows, w_out.shape[1]), BF16),
            vmem((rows, chan), BF16),
            vmem((2 * HALO, columns), F32),
            vmem((2 * HALO, chan), F32),
            vmem((rows, chan), F32),
            sem((2, 8)),
        ],
        out_specs=ANY,
    )(
        query, base, state, high, low, head, halo, taps, skips, rates, residues,
        w_near, in_hbm(w_out),
    )


def solution(mesh):
    return jax.shard_map(
        on_device,
        mesh=mesh,
        in_specs=(P("tm", None), P(), P(), P(), P(), P(), P(), P()),
        out_specs=P("tm", None),
        check_vma=False,
    )
```

```python
import functools

import jax
import jax.numpy as jnp
from jax import lax
from jax.experimental import pallas as pl
from jax.experimental.pallas import tpu as pltpu
from jax.sharding import PartitionSpec as P

F32 = jnp.float32
BF16 = jnp.bfloat16
HALO = 8
MIB = 1 << 20


def split(value):
    high = value.astype(BF16)
    return high, (value - high.astype(F32)).astype(BF16)


def dot(left, right):
    return jnp.dot(left, right, preferred_element_type=F32)


def spot(axis, count):
    shape = (1, count) if axis else (count, 1)
    return lax.broadcasted_iota(jnp.int32, shape, axis)


def copies(source, target, axis, count, sems):
    size = source.shape[axis] // count
    made = []
    for k in range(count):
        part = pl.ds(k * size, size)
        index = (part, slice(None)) if axis == 0 else (slice(None), part)
        made.append(pltpu.make_async_copy(source.at[index], target.at[index], sems.at[k]))
    return made


def column(table):
    groups, modes = table.shape
    rows = jnp.concatenate(
        [jnp.broadcast_to(table[g : g + 1, :], (modes, modes)) for g in range(groups)], axis=0
    )
    mine = spot(1, modes) == lax.rem(spot(0, groups * modes), modes)
    return jnp.sum(jnp.where(mine, rows, 0.0), axis=1, keepdims=True)


def fold(stacked, modes, per):
    width = stacked.shape[1]
    owner = spot(1, width) // per
    total = jnp.zeros((modes, width), F32)
    for g in range(stacked.shape[0] // modes):
        total = jnp.where(owner == g, stacked[g * modes : (g + 1) * modes, :], total)
    return total


def by_channel(col, modes, per, width):
    return fold(jnp.broadcast_to(col, (col.shape[0], width)), modes, per)


def feature(taps, ext, here, first, width, at=0):
    cols = slice(at, at + width)
    wide = slice(first, first + width)
    total = taps[0:1, wide] * ext[HALO + here.start : HALO + here.stop, cols]
    for k in range(1, taps.shape[0]):
        near = ext[HALO + here.start - k : HALO + here.stop - k, cols]
        total = total + taps[k : k + 1, wide] * near
    return total


EDGE = slice(0, HALO)


def multiply(hidden, inv, gain, near, total, arrive, store, late=1, count=8):
    rows, width = hidden.shape
    block = width // count
    part = rows // 3
    parts = [slice(first, first + part) for first in range(0, rows, part)]

    def made(here, k):
        cols = slice(k * block, (k + 1) * block)
        scale = jnp.concatenate([inv[here, :]] * (block // 128), axis=1)
        normed = (hidden[here, cols].astype(F32) * scale * gain[:, cols]).astype(BF16)
        return dot(normed, near(cols))

    for k in range(count - late):
        arrive(k)
        for here in parts:
            if k == 0:
                total[here, :] = made(here, k)
            else:
                total[here, :] += made(here, k)
    for here in parts:
        value = total[here, :]
        for k in range(count - late, count):
            if here.start == 0:
                arrive(k)
            value += made(here, k)
        store(here, value.astype(BF16))


def state_kernel(
    hidden_hbm, gain_hbm, w_hbm, taps_hbm, rates_hbm,
    prod_ref, inv_ref, edge_ref, own_ref, ahead_ref,
    hidden, near, gain, taps, rates, total, ext, little, sems,
):
    rows, width = hidden.shape
    chan = prod_ref.shape[1]
    reach = taps.shape[0] - 1
    small = [
        pltpu.make_async_copy(source, target, sems.at[2, k])
        for k, (source, target) in enumerate(
            ((gain_hbm, gain), (taps_hbm, taps), (rates_hbm, rates))
        )
    ]
    lines = copies(hidden_hbm, hidden, 1, 8, sems.at[0])
    weights = copies(w_hbm.at[:, pl.ds(chan, 2 * chan)], near, 0, 8, sems.at[1])
    for copy in small + lines:
        copy.start()
    inv_ref[...] = jnp.zeros_like(inv_ref)
    ext[0:HALO, :] = jnp.zeros((HALO, 2 * chan), F32)
    for copy in small:
        copy.wait()
    modes = rates.shape[1]
    left = (rows - 1 - spot(1, rows)).astype(F32)
    high, low = split(jnp.exp(-column(rates[...]) * left))
    block = width // len(lines)
    for k, copy in enumerate(lines):
        copy.wait()
        weights[k].start()

        def add(i, _, k=k):
            cols = pl.ds(pl.multiple_of(k * block + i * 256, 256), 256)
            wide = hidden[:, cols].astype(F32)
            square = wide * wide
            inv_ref[...] += square[:, :128] + square[:, 128:]
            return 0

        lax.fori_loop(0, block // 256, add, 0)
    inv = lax.rsqrt(jnp.sum(inv_ref[...], axis=1, keepdims=True) / width + 1e-06)
    inv_ref[...] = jnp.broadcast_to(inv, inv_ref.shape)
    crossed, heads = [], []

    def store(here, value):
        ext[HALO + here.start : HALO + here.stop, :] = value.astype(F32)
        key = feature(taps, ext, here, chan, chan, 0)
        value = feature(taps, ext, here, 2 * chan, chan, chan)
        product = key * value
        if here.start == 0:
            early = spot(0, HALO) < reach
            heads.extend(jnp.where(early, kind[0:HALO, :], 0.0) for kind in (key, value))
            product = jnp.where(spot(0, here.stop) >= reach, product, 0.0)
        product = product.astype(BF16)
        prod_ref[here, :] = product
        crossed.append(dot(high[:, here], product) + dot(low[:, here], product))

    deep = ahead_ref.shape[0]
    ahead = pltpu.make_async_copy(
        w_hbm.at[pl.ds(0, deep), pl.ds(0, chan)], ahead_ref, sems.at[2, 7]
    )

    def arrive(k):
        weights[k].wait()
        if k == 6:
            ahead.start()

    def weight_rows(cols):
        return near[cols, :]

    multiply(hidden, inv_ref, gain, weight_rows, total, arrive, store, late=4)

    edge_ref[0:HALO, :] = ext[HALO : 2 * HALO, :]
    edge_ref[HALO:, :] = ext[rows : rows + HALO, :]
    little[0:HALO, :] = ext[rows : rows + HALO, :]
    little[HALO:, :] = jnp.zeros((HALO, 2 * chan), F32)
    tail_k = feature(taps, little, EDGE, chan, chan, 0)
    tail_v = feature(taps, little, EDGE, 2 * chan, chan, chan)
    state = fold(sum(crossed[1:], crossed[0]), modes, chan // rates.shape[0])
    own_ref[...] = jnp.concatenate([state] + heads + [tail_k, tail_v], axis=0)
    ahead.wait()


def joined(tail_k, head_k, tail_v, head_v):
    return ((tail_k + head_k) * (tail_v + head_v)).astype(BF16).astype(F32)


def part(value, modes, k):
    return value[modes + k * HALO : modes + (k + 1) * HALO]


def merge(left, right, rate, length):
    modes = rate.shape[0]
    seam = joined(*[part(v, modes, k) for v, k in ((left, 2), (right, 0), (left, 3), (right, 1))])
    state = jnp.exp(-rate * length) * left[:modes] + right[:modes] + entering(seam, rate, length)
    return jnp.concatenate(
        [state, left[modes : modes + 2 * HALO], right[modes + 2 * HALO :]], axis=0
    )


def entering(seam, rate, length):
    total = jnp.zeros(rate.shape, F32)
    for s in range(HALO - 2):
        total += jnp.exp(-rate * (length - 1.0 - s)) * seam[s : s + 1]
    return total


def chip_kernel(place_ref, own_ref, got_ref, rates_ref, first_ref, chip_ref, *, hop, per):
    zero = place_ref[0:1, :] == 0
    own, got = own_ref[...], got_ref[...]
    first = jnp.where(zero, own, got)
    second = jnp.where(zero, got, own)
    modes, width = first_ref.shape
    rate = by_channel(column(rates_ref[...]), modes, per, width)
    first_ref[...] = first[:modes]
    chip_ref[...] = merge(first, second, rate, hop)


def line_kernel(place_ref, own_ref, *refs, hop, reach, per, along):
    got_refs, (rates_ref, tail_ref, spread_ref, inner_ref, early_ref, sent_ref) = (
        refs[: along - 1], refs[along - 1 :]
    )
    sent_ref[...] = tail_ref[...]
    own = own_ref[...]
    modes = rates_ref.shape[1]
    rate = by_channel(column(rates_ref[...]), modes, per, own.shape[1])
    spot_x = place_ref[1:2, :]
    chips = []
    for j in range(along):
        chip = own
        for m in range(1, along):
            chip = jnp.where(spot_x == (j ^ m), got_refs[m - 1][...], chip)
        chips.append(chip)
    total = chips[0]
    before = jnp.zeros_like(total)
    for j in range(1, along):
        before = jnp.where(spot_x == j, total, before)
        total = merge(total, chips[j], rate, 2.0 * hop)
    inner_ref[...] = before
    early_ref[...] = own[modes : modes + 2 * HALO]
    pieces = [total[:modes]] + [part(total, modes, k)[:reach] for k in range(4)]
    packed = jnp.concatenate(pieces, axis=0).astype(BF16)
    spread_ref[...] = jnp.broadcast_to(packed[None], spread_ref.shape)


def query_kernel(
    after_ref, hidden_hbm, gain_ref, w_hbm, taps_ref, inv_ref, edge_ref, ahead_ref,
    query_ref, head_ref, tail_ref, hidden, near, total, ext, sems,
):
    rows, width = hidden.shape
    chan = query_ref.shape[1]
    deep, rest = ahead_ref.shape[0], near.shape[0]
    count = 8
    known = count * deep // width
    lines = copies(hidden_hbm, hidden, 1, count, sems.at[0])
    source = w_hbm.at[pl.ds(deep, rest), pl.ds(0, chan)]
    weights = copies(source, near, 0, count - known, sems.at[1])
    for k, line in enumerate(lines):
        line.start()
        if k >= known:
            weights[k - known].start()

    def arrive(k):
        lines[k].wait()
        if k >= known:
            weights[k - known].wait()

    def weight_rows(cols):
        if cols.stop <= deep:
            return ahead_ref[cols, :]
        return near[cols.start - deep : cols.stop - deep, :]

    def store(here, value):
        ext[HALO + here.start : HALO + here.stop, :] = value.astype(F32)
        query_ref[here, :] = feature(taps_ref, ext, here, 0, chan, 0)

    ext[0:HALO, :] = jnp.zeros((HALO, chan), F32)
    multiply(hidden, inv_ref, gain_ref, weight_rows, total, arrive, store)
    head_ref[:, :chan] = ext[HALO : 2 * HALO, :]
    head_ref[:, chan:] = edge_ref[0:HALO, :]
    tail = jnp.concatenate([ext[rows : rows + HALO, :], edge_ref[HALO:, :]], axis=1)
    tail_ref[...] = tail.astype(BF16)


def local_kernel(
    after_ref, prod_ref, skip_ref, rates_ref, residues_ref, rrow_ref, wrow_ref, w_hbm,
    base_ref, high_ref, low_ref, near_ref, rise_ref, above_ref, sem,
):
    fetch = pltpu.make_async_copy(w_hbm.at[:, pl.ds(0, near_ref.shape[1])], near_ref, sem)
    fetch.start()
    rows, chan = prod_ref.shape
    groups, modes = rates_ref.shape
    times = spot(0, rows).astype(F32) + 1.0
    high, low = split(wrow_ref[...] * jnp.exp(-rrow_ref[...] * times))
    high_ref[...] = high
    low_ref[...] = low
    rcol = column(rates_ref[...])
    wcol = column(residues_ref[...]) * jnp.sqrt(2.0 * rcol)
    block = 128
    per = chan // groups
    places = [slice(first, first + block) for first in range(0, rows, block)]
    for here in places:
        base_ref[here, :] = skip_ref[...] * prod_ref[here, :].astype(F32)

    keep = spot(1, chan) // per == spot(0, groups * modes) // modes
    leave_high, leave_low = split(jnp.exp(-rcol * (block - 1 - spot(1, block)).astype(F32)))
    fall = jnp.exp(-rcol * float(block))
    state = jnp.zeros((groups * modes, chan), F32)
    for here, following in zip(places, places[1:]):
        mine = prod_ref[here, :]
        state = fall * state + (dot(leave_high, mine) + dot(leave_low, mine))
        near_high, near_low = split(jnp.where(keep, state, 0.0))
        rise = high[:block, :]
        base_ref[following, :] += (
            dot(rise, near_high) + dot(low[:block, :], near_high) + dot(rise, near_low)
        )

    span = 2 * block
    spots = spot(1, span)
    lags = jnp.where(spots == 0, 0, span - spots)
    terms = wcol * jnp.exp(-rcol * lags.astype(F32))
    terms = jnp.where((spots == 0) | (spots > block), terms, 0.0)
    for g in range(groups):
        filt = jnp.sum(terms[g * modes : (g + 1) * modes, :], axis=0, keepdims=True)
        wide = jnp.broadcast_to(filt, (block, span))
        square = pltpu.roll(wide, 0, 1, stride=1, stride_axis=0)[:, :block].astype(BF16)
        cols = slice(g * per, (g + 1) * per)
        for here in places:
            base_ref[here, cols] += dot(square, prod_ref[here, cols])
    rate = by_channel(rcol, modes, per, chan)
    weight = by_channel(wcol, modes, per, chan)
    reach = rise_ref.shape[0] // modes
    for s in range(reach):
        rise_ref[s * modes : (s + 1) * modes, :] = jnp.exp(rate * (s + 1.0))
    for s in range(HALO):
        above = jnp.sum(weight * jnp.exp(rate * float(s)), axis=0, keepdims=True)
        above_ref[s : s + 1, :] = above
    fetch.wait()


def prefix_kernel(
    place_ref, all_ref, rates_ref, first_ref, inner_ref, early_ref, after_ref,
    state_ref, seams, tails, *, hop, reach, per, along,
):
    count = all_ref.shape[0]
    modes, width = state_ref.shape
    zero, spot_x, line = place_ref[0:1, :] == 0, place_ref[1:2, :], place_ref[2:3, :]
    col = column(rates_ref[...])
    rate = by_channel(col, modes, per, width)
    span = 2.0 * hop * along
    fall = jnp.exp(-rate * span)
    wide = all_ref[...].astype(F32)

    def piece(k):
        return wide[:, modes + k * reach : modes + (k + 1) * reach, :]

    def before(k):
        value = piece(k)
        return jnp.concatenate([jnp.zeros_like(value[:1]), value[:-1]], axis=0)

    seams[...] = jnp.zeros_like(seams)
    tails[...] = jnp.zeros_like(tails)
    tail_k, tail_v = before(2), before(3)
    tails[:, 0:reach, :] = tail_k
    tails[:, HALO : HALO + reach, :] = tail_v
    seams[:, 0:reach, :] = joined(tail_k, piece(0), tail_v, piece(1))
    total = jnp.zeros((modes, width), F32)
    for j in range(count):
        total = jnp.where(j < line, fall * total + wide[j, :modes, :], total)
    index = spot(1, count * HALO)
    place, step = index // HALO, lax.rem(index, HALO)
    level = line[:, : count * HALO]
    lag = span * (level - 1 - place).astype(F32) + (span - 1.0) - step.astype(F32)
    fade = jnp.where(place < level, jnp.exp(-col * jnp.maximum(lag, 0.0)), 0.0)
    high, low = split(fade)
    products = seams[...].reshape(count * HALO, width).astype(BF16)
    total += fold(dot(high, products) + dot(low, products), modes, per)

    inner, early = inner_ref[...], early_ref[...]
    outer = tails[0]
    for j in range(1, count):
        outer = jnp.where(line == j, tails[j], outer)
    heads = [part(inner, modes, k) for k in (0, 1)]
    seam = joined(outer[:HALO], heads[0], outer[HALO:], heads[1])
    length = 2.0 * hop * spot_x.astype(F32)
    within = jnp.exp(-rate * length) * total + inner[:modes]
    for s in range(reach):
        within += jnp.exp(-rate * jnp.maximum(length - 1.0 - s, 0.0)) * seam[s : s + 1]
    starts = spot_x == 0
    total = jnp.where(starts, total, within)
    last_k = jnp.where(starts, outer[:HALO], part(inner, modes, 2))
    last_v = jnp.where(starts, outer[HALO:], part(inner, modes, 3))
    seam = joined(last_k, early[:HALO], last_v, early[HALO:])
    following = jnp.exp(-rate * hop) * total + first_ref[...] + entering(seam, rate, hop)
    state_ref[...] = jnp.where(zero, total, following)


def mix_kernel(
    query_ref, base_ref, state_ref, high_ref, low_ref, head_ref, halo_ref,
    taps_ref, skip_ref, lift_ref, above_ref, near_ref, w_hbm,
    out_hbm, w_ref, staged, gated, ext, shift, sums, sems,
):
    steps = sems.shape[1]
    kept = near_ref.shape[1]
    block = out_hbm.shape[1] // steps
    rest = w_ref.shape[1]
    weights = copies(w_hbm.at[:, pl.ds(kept, rest)], w_ref, 1, rest // block, sems.at[0])
    for copy in weights:
        copy.start()
    rows, chan = query_ref.shape
    modes = state_ref.shape[0]
    groups = high_ref.shape[1] // modes
    per = chan // groups
    reach = taps_ref.shape[0] - 1
    ext[0:HALO, :] = halo_ref[...].astype(F32)
    ext[HALO:, :] = head_ref[...]
    query, key, value = [feature(taps_ref, ext, EDGE, n * chan, chan, n * chan) for n in range(3)]
    product = jnp.where(spot(0, HALO) < reach, key * value, 0.0).astype(BF16).astype(F32)
    shift[0:HALO, :] = product
    shift[HALO:, :] = jnp.zeros((HALO, chan), F32)
    state = state_ref[...]
    for s in range(reach):
        state += lift_ref[s * modes : (s + 1) * modes, :] * product[s : s + 1, :]
    owner = spot(1, chan) // per
    spread = jnp.concatenate([jnp.where(owner == g, state, 0.0) for g in range(groups)], axis=0)
    high, low = split(spread)
    rise = high_ref[...]
    sums[...] = base_ref[...] + (dot(rise, high) + dot(low_ref[...], high) + dot(rise, low))
    start = sums[0:HALO, :] + skip_ref[...] * product
    for ahead in range(1, reach):
        start -= above_ref[ahead : ahead + 1, :] * shift[ahead : ahead + HALO, :]
    sums[...] = query_ref[...] * sums[...]
    sums[0:HALO, :] = query * start
    gated[...] = sums[...].astype(BF16)

    sent = copies(staged, out_hbm, 1, steps, sems.at[1])
    for k in range(steps):
        source, first = near_ref, k * block
        if first >= kept:
            source, first = w_ref, first - kept
            weights[first // block].wait()
        made = dot(gated[...], source[:, first : first + block])
        staged[:, k * block : (k + 1) * block] = made.astype(BF16)
        sent[k].start()
    for copy in sent:
        copy.wait()


VMEM = pl.BlockSpec(memory_space=pltpu.VMEM)
ANY = pl.BlockSpec(memory_space=pl.ANY)


def call(kernel, name, specs, outs, scratch=(), limit=40, flops=0, size=0, out_specs=None):
    return pl.pallas_call(
        kernel,
        in_specs=specs,
        out_specs=out_specs or [VMEM] * len(outs),
        out_shape=outs,
        scratch_shapes=list(scratch),
        compiler_params=pltpu.CompilerParams(vmem_limit_bytes=limit * MIB),
        cost_estimate=pl.CostEstimate(flops=flops, bytes_accessed=size, transcendentals=0),
        name=name,
    )


def in_hbm(value):
    return pltpu.with_memory_space_constraint(value, pltpu.HBM)


def on_device(hidden, norm_gain, w_in, w_short, residues, rates, skip, w_out):
    rows, width = hidden.shape
    columns = w_in.shape[1]
    chan = columns // 3
    groups, modes = rates.shape
    per = chan // groups
    reach = w_short.shape[1] - 1
    devices = lax.axis_size("tm")
    here = lax.axis_index("tm")
    along = 4
    place = jnp.stack([here % 2, here // 2 % along, here // (2 * along)]).astype(jnp.int32)
    place = jnp.broadcast_to(place[:, None], (3, chan))
    gain = norm_gain[None, :]
    taps = w_short.T
    skips = skip[None, :]
    vmem, sem = pltpu.VMEM, pltpu.SemaphoreType.DMA

    deep = width // 2
    product, inv, edges, own, ahead = call(
        state_kernel,
        "state",
        [ANY] * 5,
        [
            vmem((rows, chan), BF16),
            vmem((rows, 128), F32),
            vmem((2 * HALO, 2 * chan), F32),
            vmem((modes + 4 * HALO, chan), F32),
            vmem((deep, chan), BF16),
        ],
        [
            vmem((rows, width), BF16),
            vmem((width, 2 * chan), BF16),
            vmem((1, width), F32),
            vmem((reach + 1, columns), F32),
            vmem((groups, modes), F32),
            vmem((rows, 2 * chan), F32),
            vmem((HALO + rows, 2 * chan), F32),
            vmem((2 * HALO, 2 * chan), F32),
            sem((3, 8)),
        ],
        flops=4 * rows * width * chan,
        size=2 * width * (rows + 2 * chan),
    )(in_hbm(hidden), in_hbm(gain), in_hbm(w_in), in_hbm(taps), in_hbm(rates))

    pairs = [(i, i ^ 1) for i in range(devices)]
    got = lax.ppermute(own, "tm", pairs)
    first, chip = call(
        functools.partial(chip_kernel, hop=float(rows), per=per),
        "chip",
        [VMEM] + [VMEM] * 3,
        [vmem((modes, chan), F32), vmem((modes + 4 * HALO, chan), F32)],
    )(place, own, got, rates)
    lines = [
        lax.ppermute(chip, "tm", [(i, i ^ (2 * m)) for i in range(devices)])
        for m in range(1, along)
    ]

    query, head, tail = call(
        query_kernel,
        "query",
        [VMEM, ANY, VMEM, ANY] + [VMEM] * 4,
        [vmem((rows, chan), F32), vmem((HALO, columns), F32), vmem((HALO, columns), BF16)],
        [
            vmem((rows, width), BF16),
            vmem((width - deep, chan), BF16),
            vmem((rows, chan), F32),
            vmem((HALO + rows, chan), F32),
            sem((2, 8)),
        ],
        flops=2 * rows * width * chan,
        size=2 * width * (rows + chan),
    )(first, in_hbm(hidden), gain, in_hbm(w_in), taps, inv, edges, ahead)
    spread, inner, early, tail = call(
        functools.partial(line_kernel, hop=float(rows), reach=reach, per=per, along=along),
        "line",
        [VMEM] + [VMEM] * (along + 2),
        [
            jax.ShapeDtypeStruct((devices // 2 // along, modes + 4 * reach, chan), BF16),
            vmem((modes + 4 * HALO, chan), F32),
            vmem((2 * HALO, chan), F32),
            vmem((HALO, columns), BF16),
        ],
    )(place, chip, *lines, rates, tail)
    members = [list(range(c, devices, 2 * along)) for c in range(2 * along)]
    gathered = lax.all_to_all(spread, "tm", 0, 0, tiled=True, axis_index_groups=members)
    halo = lax.ppermute(tail, "tm", [(i, i + 1) for i in range(devices - 1)])

    weights = residues * jnp.sqrt(2.0 * rates)
    kept = w_out.shape[1] * 3 // 8
    base, high, low, w_near, lift, above = call(
        local_kernel,
        "local",
        [VMEM] * 7 + [ANY],
        [
            vmem((rows, chan), F32),
            vmem((rows, groups * modes), BF16),
            vmem((rows, groups * modes), BF16),
            vmem((chan, kept), BF16),
            vmem((reach * modes, chan), F32),
            vmem((HALO, chan), F32),
        ],
        [sem],
        flops=2 * rows * rows * chan,
        size=6 * rows * chan,
    )(
        tail, product, skips, rates, residues, rates.reshape(1, -1), weights.reshape(1, -1),
        in_hbm(w_out),
    )

    state, = call(
        functools.partial(prefix_kernel, hop=float(rows), reach=reach, per=per, along=along),
        "prefix",
        [VMEM] + [VMEM] * 6,
        [vmem((modes, chan), F32)],
        [
            vmem((devices // 2 // along, HALO, chan), F32),
            vmem((devices // 2 // along, 2 * HALO, chan), F32),
        ],
    )(place, gathered, rates, first, inner, early, low)

    return call(
        mix_kernel,
        "mix",
        [VMEM] * 12 + [ANY],
        jax.ShapeDtypeStruct((rows, w_out.shape[1]), BF16),
        [
            vmem((chan, w_out.shape[1] - kept), BF16),
            vmem((rows, w_out.shape[1]), BF16),
            vmem((rows, chan), BF16),
            vmem((2 * HALO, columns), F32),
            vmem((2 * HALO, chan), F32),
            vmem((rows, chan), F32),
            sem((2, 8)),
        ],
        out_specs=ANY,
    )(
        query, base, state, high, low, head, halo, taps, skips, lift, above,
        w_near, in_hbm(w_out),
    )


def solution(mesh):
    return jax.shard_map(
        on_device,
        mesh=mesh,
        in_specs=(P("tm", None), P(), P(), P(), P(), P(), P(), P()),
        out_specs=P("tm", None),
        check_vma=False,
    )
```
